256 devices in a mesh: seq: 64 (over z_hi, y, x), head: 4 (over z_lo, core).
Axes of the slice: x: 4, y: 4, z: 8 (z_hi: 4, z_lo: 2; z = z_hi * 2 + z_lo), core: 2. Of those that a mesh axis runs over, the one named last changes fastest.
Arguments:
- queries: bfloat16 [16384, 20, 128], P(('seq', 'head')), may hold values from -6 to 6
- key_vectors: bfloat16 [16384, 20, 128], P(('seq', 'head')), may hold values from -6 to 6
- value_vectors: bfloat16 [16384, 20, 128], P(('seq', 'head')), may hold values from -40 to 40
- grad_output: bfloat16 [16384, 20, 128], P(('seq', 'head')), may hold values from -40 to 40
- block_mask: int32 [128, 128], replicated, may hold values from 0 to 1, as said below
- block_frame: int32 [128], replicated, may hold values from 0 to 20, as said below
Outputs:
- attended: bfloat16 [16384, 20, 128], P(('seq', 'head'))
- grad_queries: bfloat16 [16384, 20, 128], P(('seq', 'head'))
- grad_keys: bfloat16 [16384, 20, 128], P(('seq', 'head'))
- grad_values: bfloat16 [16384, 20, 128], P(('seq', 'head'))
The draws below stay inside these ranges and needn't reach their ends.
Inputs may be any that keep to these rules, and one draw needn't show every extreme that they name: Frame groups are runs of 2 blocks. block_mask is 1 on the diagonal, and 0 unless the frame groups of its row and column are equal or differ by a power of two. `block_frame`: Nondecreasing; block 0 lies in frame 0 and the last block in frame 21 - 1.
All inputs are finite; a program needn't handle non-finite values.
Results may differ from the reference program's by a relative error of at most 0.038.
Values may be sent and summed in bfloat16 or wider, within the bound.
No kernel may reach another device: no remote copies, remote signals or barrier semaphores. Data moves between devices by JAX's collectives and lax.ppermute only.
A program may use at most 128 MiB of HBM per device.

```python
import math
import jax
import jax.numpy as jnp
from jax import lax

H = 20
E = 128
ROT = 44
BLK = 128
FRAMES = 21
TOK_SEQ = 256
S = 16384
NB = 128
N_SEQ = 64


def shared_rows(key):
    base_query = jnp.clip(jax.random.normal(jax.random.fold_in(key, 21), (S, H, E), jnp.float32), -5.5, 5.5)
    base_key = jnp.clip(jax.random.normal(jax.random.fold_in(key, 22), (S, H, E), jnp.float32), -5.5, 5.5)
    return (base_query, base_key)


def draw_queries(key, part):
    base_query, base_key = shared_rows(key)
    return base_query.astype(jnp.bfloat16)


def draw_key_vectors(key, part):
    base_query, base_key = shared_rows(key)
    return base_key.astype(jnp.bfloat16)


def draw_block_mask(key, part):
    key = jax.random.fold_in(key, 5)
    per_group = TOK_SEQ // BLK
    group_of = jnp.arange(NB, dtype=jnp.int32) // per_group
    group_gap = jnp.abs(group_of[:, None] - group_of[None, :])
    is_power = group_gap & group_gap - 1 == 0
    chance = jnp.where(group_gap <= 1, 75, 50)
    dice_roll = jax.random.randint(key, (NB, NB), 0, 100)
    kept_pair = (dice_roll < chance) & is_power
    diagonal = jnp.eye(NB, dtype=bool)
    return (kept_pair | diagonal).astype(jnp.int32)


def draw_block_frame(key, part):
    key = jax.random.fold_in(key, 9)
    jitter = jax.random.randint(key, (NB,), 0, NB)
    index = jnp.arange(NB, dtype=jnp.int32)
    frame_ids = jnp.minimum((index * FRAMES + jitter) // NB, FRAMES - 1)
    frame_ids = lax.cummax(frame_ids, axis=0)
    return jnp.where(index == NB - 1, FRAMES - 1, frame_ids).astype(jnp.int32)


def block_scale(stream_key, extent, shards, least, top_value):
    factor_of, own = 1.0, jax.random.fold_in(stream_key, 6)
    for position, parts in shards:
        steps = jnp.exp(jax.random.uniform(jax.random.fold_in(own, position), (parts,), jnp.float32, least / len(shards), top_value / len(shards)))
        factor_of = factor_of * jnp.repeat(steps, extent[position] // parts).reshape([-1 if axis == position else 1 for axis in range(len(extent))])
    return factor_of


def centred(rng, dims, scale, bound, split=(), held_as=jnp.bfloat16):
    gain = block_scale(rng, dims, split, -0.22, 0.18) if split else 1.0
    array = jax.random.normal(rng, dims, jnp.float32) * scale * gain
    return jnp.minimum(jnp.maximum(array, -bound), bound).astype(held_as)


def setup_inputs(seed: int = 0) -> dict:
    splits = jax.random.split(jax.random.key(seed), 7)
    return {
        "queries": draw_queries(jax.random.fold_in(splits[6], 71), 0),
        "key_vectors": draw_key_vectors(jax.random.fold_in(splits[6], 71), 0),
        "value_vectors": centred(splits[2], (S, H, E), 8.0, 40.0, ((0, 256),)),
        "grad_output": centred(splits[3], (S, H, E), 8.0, 40.0, ((0, 256),)),
        "block_mask": draw_block_mask(jax.random.fold_in(splits[6], 71), 0),
        "block_frame": draw_block_frame(jax.random.fold_in(splits[6], 71), 0),
    }


def signed_offsets(count):
    found = [0]
    stride = 1
    while stride < count:
        found = found + [stride, -stride]
        stride = stride * 2
    return found

def rotate(values_in, frame_rows, inverse):
    half_dims = ROT // 2
    inv_freq = 10000.0 ** (-2.0 * jnp.arange(half_dims, dtype=jnp.float32) / ROT)
    angles = frame_rows.astype(jnp.float32)[:, None] * inv_freq[None, :]
    cosine = jnp.cos(angles)[:, None, :]
    sine_part = jnp.sin(angles)[:, None, :]
    if inverse:
        sine_part = -sine_part
    first_half = values_in[..., :half_dims]
    second_half = values_in[..., half_dims:ROT]
    return jnp.concatenate([first_half * cosine - second_half * sine_part, first_half * sine_part + second_half * cosine, values_in[..., ROT:]], axis=-1)

def pair_allow(block_mask, row_group, col_group):
    per_group = TOK_SEQ // BLK
    inside = ((row_group >= 0) & (row_group < N_SEQ) & (col_group >= 0) & (col_group < N_SEQ)).astype(jnp.int32)
    row_start = jnp.clip(row_group, 0, N_SEQ - 1).astype(jnp.int32) * per_group
    col_start = jnp.clip(col_group, 0, N_SEQ - 1).astype(jnp.int32) * per_group
    block_piece = lax.dynamic_slice(block_mask, (row_start, col_start), (per_group, per_group)) * inside
    expanded = jnp.broadcast_to(block_piece[:, None, :, None], (per_group, BLK, per_group, BLK))
    return expanded.reshape(TOK_SEQ, TOK_SEQ) > 0

def reference(queries, key_vectors, value_vectors, grad_output, block_mask, block_frame):
    score_scale = 1.0 / math.sqrt(E)
    frame_rows = jnp.repeat(block_frame, BLK)
    q_rot = rotate(queries.astype(jnp.float32), frame_rows, False).astype(jnp.bfloat16)
    k_rot = rotate(key_vectors.astype(jnp.float32), frame_rows, False).astype(jnp.bfloat16)
    q_groups = q_rot.reshape(N_SEQ, TOK_SEQ, H, E)
    k_groups = k_rot.reshape(N_SEQ, TOK_SEQ, H, E)
    v_groups = value_vectors.reshape(N_SEQ, TOK_SEQ, H, E)
    g_groups = grad_output.reshape(N_SEQ, TOK_SEQ, H, E)
    offsets = signed_offsets(N_SEQ)
    group_ids = jnp.arange(N_SEQ, dtype=jnp.int32)

    def collect(stacked, center, sign, axis_at):
        return jnp.concatenate([stacked[jnp.clip(center + sign * offset, 0, N_SEQ - 1)] for offset in offsets], axis=axis_at)

    def forward_group(center):
        keys_cat = collect(k_groups, center, -1, 0)
        vals_cat = collect(v_groups, center, -1, 0)
        allowed = jnp.concatenate([pair_allow(block_mask, center, center - offset) for offset in offsets], axis=1)
        scores = jnp.einsum('qhe,khe->hqk', q_groups[center].astype(jnp.float32), keys_cat.astype(jnp.float32)) * score_scale
        masked = jnp.where(allowed[None], scores, -1e+30)
        running = lax.optimization_barrier(jnp.max(masked, axis=2))
        denominator = lax.optimization_barrier(jnp.sum(jnp.exp(masked - running[:, :, None]), axis=2))
        log_total = running + jnp.log(denominator)
        weights_bf = jnp.exp(masked - log_total[:, :, None]).astype(jnp.bfloat16)
        attended_g = jnp.einsum('hqk,khe->qhe', weights_bf.astype(jnp.float32), vals_cat.astype(jnp.float32)).astype(jnp.bfloat16)
        return (attended_g, log_total)
    attended_groups, log_totals = lax.map(forward_group, group_ids)
    row_delta = lax.optimization_barrier(jnp.sum(g_groups.astype(jnp.float32) * attended_groups.astype(jnp.float32), axis=3)).transpose(0, 2, 1)

    def query_grads(center):
        keys_cat = collect(k_groups, center, -1, 0)
        vals_cat = collect(v_groups, center, -1, 0)
        allowed = jnp.concatenate([pair_allow(block_mask, center, center - offset) for offset in offsets], axis=1)
        scores = jnp.einsum('qhe,khe->hqk', q_groups[center].astype(jnp.float32), keys_cat.astype(jnp.float32)) * score_scale
        weights = jnp.exp(jnp.where(allowed[None], scores - log_totals[center][:, :, None], -1e+30))
        dweights = jnp.einsum('qhe,khe->hqk', g_groups[center].astype(jnp.float32), vals_cat.astype(jnp.float32))
        dscore = (weights * (dweights - row_delta[center][:, :, None])).astype(jnp.bfloat16)
        return jnp.einsum('hqk,khe->qhe', dscore.astype(jnp.float32), keys_cat.astype(jnp.float32)) * score_scale

    def key_grads(center):
        grad_k = jnp.zeros((TOK_SEQ, H, E), jnp.float32)
        grad_v = jnp.zeros((TOK_SEQ, H, E), jnp.float32)
        key_rows = k_groups[center].astype(jnp.float32)
        value_rows = v_groups[center].astype(jnp.float32)
        for offset in offsets:
            source = center + offset
            clipped = jnp.clip(source, 0, N_SEQ - 1)
            query_rows = q_groups[clipped].astype(jnp.float32)
            grad_rows = g_groups[clipped].astype(jnp.float32)
            totals = log_totals[clipped]
            deltas = row_delta[clipped]
            allowed = pair_allow(block_mask, source, center)
            scores = jnp.einsum('qhe,khe->hqk', query_rows, key_rows) * score_scale
            weights = jnp.exp(jnp.where(allowed[None], scores - totals[:, :, None], -1e+30))
            dweights = jnp.einsum('qhe,khe->hqk', grad_rows, value_rows)
            dscore = (weights * (dweights - deltas[:, :, None])).astype(jnp.bfloat16)
            term_k = jnp.einsum('hqk,qhe->khe', dscore.astype(jnp.float32), query_rows)
            term_v = jnp.einsum('hqk,qhe->khe', weights.astype(jnp.bfloat16).astype(jnp.float32), grad_rows)
            if offset != 0:
                term_k = lax.optimization_barrier(term_k.astype(jnp.bfloat16)).astype(jnp.float32)
                term_v = lax.optimization_barrier(term_v.astype(jnp.bfloat16)).astype(jnp.float32)
            grad_k = grad_k + term_k
            grad_v = grad_v + term_v
        return (grad_k * score_scale, grad_v)
    dq_groups = lax.map(query_grads, group_ids)
    dk_groups, dv_groups = lax.map(key_grads, group_ids)
    attended = attended_groups.reshape(S, H, E)
    grad_queries = rotate(dq_groups.reshape(S, H, E), frame_rows, True).astype(jnp.bfloat16)
    grad_keys = rotate(dk_groups.reshape(S, H, E), frame_rows, True).astype(jnp.bfloat16)
    grad_values = dv_groups.reshape(S, H, E).astype(jnp.bfloat16)
    return (attended, grad_queries, grad_keys, grad_values)
```

```python
import functools
import math

import jax
import jax.numpy as jnp
import numpy as np
from jax import lax
from jax.experimental import pallas as pl
from jax.experimental.pallas import tpu as pltpu
from jax.sharding import Mesh, PartitionSpec as P

ROT = 44
HALF = ROT // 2
BLK = 128
E = 128
TOK = 256
QTR = 64
GROUPS = 64
PLANE = 16
ZG = 4
UNITS = 5
NEG = -1e30
SHIFTS = (1, -1, 2, -2, 4, -4, 8)
OFFSETS = (0, 1, -1, 2, -2, 4, -4, 8, -8, 16, -16, 32, -32)
OWN = 36
ABOVE = 42
SLOTS = 45
SCALE = 1.0 / math.sqrt(E)
LOG2E = 1.4426950408889634
COEF = SCALE * LOG2E
F32 = jnp.float32
BF16 = jnp.bfloat16
ANY = pl.BlockSpec(memory_space=pl.ANY)
SMEM = pl.BlockSpec(memory_space=pltpu.SMEM)
VMEM = pl.BlockSpec(memory_space=pltpu.VMEM)


def dot(a, b, ca, cb):
    return lax.dot_general(a, b, (((ca,), (cb,)), ((), ())), preferred_element_type=F32)


def turn(x, c, s1, s2):
    return x * c + pltpu.roll(x, HALF, x.ndim - 1) * s1 + pltpu.roll(x, E - HALF, x.ndim - 1) * s2


def pack_kernel(pos, tab, a_ref, b_ref, m_ref, x_ref):
    row = 2 * pos[0] + pos[2] // 2
    t = tab[row]
    a = turn(a_ref[...].astype(F32), t[0:1][None], t[1:2][None], t[2:3][None])
    a = jnp.swapaxes(a, 0, 1).astype(BF16)
    b = jnp.swapaxes(b_ref[...].astype(F32), 0, 1).astype(BF16)
    m_ref[:, 0] = a[:16]
    m_ref[:, 1] = b[:16]
    x_ref[:, 0] = a[16:]
    x_ref[:, 1] = b[16:]


def pack(pos, tab, a, b):
    return pl.pallas_call(
        pack_kernel,
        out_shape=(
            jax.ShapeDtypeStruct((16, 2, QTR, E), BF16),
            jax.ShapeDtypeStruct((4, 2, QTR, E), BF16),
        ),
        in_specs=[SMEM, VMEM, VMEM, VMEM],
        out_specs=(VMEM, VMEM),
        compiler_params=pltpu.CompilerParams(vmem_limit_bytes=40 * 2**20),
        name="pack",
    )(pos, tab, a, b)


def unpack_kernel(m_ref, x_ref, a_ref, b_ref):
    for i, o in ((0, a_ref), (1, b_ref)):
        v = jnp.concatenate([m_ref[:, i], x_ref[:, i]], axis=0).astype(F32)
        o[...] = jnp.swapaxes(v, 0, 1).astype(BF16)


def unpack(m, x):
    shape = jax.ShapeDtypeStruct((QTR, 20, E), BF16)
    return pl.pallas_call(
        unpack_kernel,
        out_shape=(shape, shape),
        in_specs=[VMEM, VMEM],
        out_specs=(VMEM, VMEM),
        compiler_params=pltpu.CompilerParams(vmem_limit_bytes=40 * 2**20),
        name="unpack",
    )(m, x)


def source(offset, unit, zh, p):
    is_x = unit == 4
    z = jnp.where(is_x, zh, unit)
    group = z * PLANE + p
    other = group - offset
    valid = (other >= 0) & (other < GROUPS)
    if offset == 0:
        slot = OWN + jnp.where(is_x, 0, 1 + z)
    elif abs(offset) >= PLANE:
        m = OWN + 1 + jnp.clip(z - offset // PLANE, 0, ZG - 1)
        x = {16: ABOVE, -16: ABOVE + 1}.get(offset, ABOVE + 2)
        slot = jnp.where(is_x, x, m)
    else:
        at = p - offset
        w = jnp.where((at < 0) | (at >= PLANE), 1, 0)
        step = jnp.where(at < 0, -1, jnp.where(at >= PLANE, 1, 0))
        zz = jnp.clip(z + step, 0, ZG - 1)
        if abs(offset) < 8:
            slot = 5 * SHIFTS.index(offset) + jnp.where(is_x, 4 * w, zz + 1 - w)
        else:
            slot = 30 + jnp.where(is_x, 5 * w, 1 + zz)
    return group, jnp.clip(other, 0, GROUPS - 1), valid, slot


def add_bias(st, bias):
    top = jnp.concatenate([st[:BLK, :BLK] + bias[0][0], st[:BLK, BLK:] + bias[0][1]], axis=1)
    low = jnp.concatenate([st[BLK:, :BLK] + bias[1][0], st[BLK:, BLK:] + bias[1][1]], axis=1)
    return jnp.concatenate([top, low], axis=0)


def bias_of(mask, q_group, k_group, valid):
    return [
        [
            jnp.where(valid & (mask[2 * q_group + qb, 2 * k_group + kb] != 0), 0.0, NEG)
            for qb in range(2)
        ]
        for kb in range(2)
    ]


def fetch(parts, pool, sems):
    at = 0
    copies = []
    for n, ref in enumerate(parts):
        copy = pltpu.make_async_copy(ref, pool.at[pl.ds(at, ref.shape[0])], sems.at[n])
        copy.start()
        copies.append(copy)
        at += ref.shape[0]
    for copy in copies:
        copy.wait()


def rows_of(ref, *index):
    return ref[index[0], :, index[1]].reshape(TOK, E)


def unturn(x, tab, z):
    halves = []
    for blk in range(2):
        t = tab[2 * z + blk]
        halves.append(turn(x[blk * BLK : (blk + 1) * BLK], t[0:1], -t[1:2], -t[2:3]))
    return jnp.concatenate(halves, axis=0)


def put(unit, m_ref, x_ref, which, val):
    for b in range(4):
        piece = val[b * QTR : (b + 1) * QTR]

        @pl.when(unit < 4)
        def _():
            m_ref[unit * 4 + b, which] = piece

        @pl.when(unit == 4)
        def _():
            x_ref[b, which] = piece


def query_kernel(pos, mask, tab, *refs):
    parts, qg = refs[:11], refs[11]
    m_ref, x_ref, stats, pool, sems, scores = refs[12:]
    fetch(parts, pool, sems)
    zh, p = pos[0], pos[1]

    def body(unit, carry):
        z = jnp.where(unit == 4, zh, unit)
        own = jnp.where(unit == 4, 0, unit + 1)
        q = rows_of(qg, own, 0)
        g = rows_of(qg, own, 1)
        gt = jnp.transpose(g.astype(F32))
        slots = []
        top = jnp.full((1, TOK), NEG, F32)
        for n, offset in enumerate(OFFSETS):
            group, other, valid, slot = source(offset, unit, zh, p)
            slots.append(slot)
            st = add_bias(dot(rows_of(pool, slot, 0), q, 1, 1), bias_of(mask, group, other, valid))
            scores[n] = st
            top = jnp.maximum(top, jnp.max(st, axis=0, keepdims=True))
        top = top * COEF
        total = jnp.zeros((1, TOK), F32)
        out = jnp.zeros((E, TOK), F32)
        for n in range(len(OFFSETS)):
            w = jnp.exp2(scores[n] * COEF - top)
            scores[n] = w
            total = total + jnp.sum(w, axis=0, keepdims=True)
            out = out + dot(rows_of(pool, slots[n], 1), w.astype(BF16), 0, 0)
        inv = 1.0 / total
        att = (out * inv).astype(BF16)
        delta = jnp.sum(gt * att.astype(F32), axis=0, keepdims=True)
        stats[pl.ds(2 * unit, 1), :] = top + jnp.log2(total)
        stats[pl.ds(2 * unit + 1, 1), :] = delta
        dq = jnp.zeros((E, TOK), F32)
        for n in range(len(OFFSETS)):
            dp = dot(rows_of(pool, slots[n], 1), g, 1, 1)
            ds = (scores[n] * inv * (dp - delta)).astype(BF16)
            dq = dq + dot(rows_of(pool, slots[n], 0), ds, 0, 0)
        put(unit, m_ref, x_ref, 0, jnp.transpose(att.astype(F32)).astype(BF16))
        put(unit, m_ref, x_ref, 1, unturn(jnp.transpose(dq * SCALE), tab, z).astype(BF16))
        return carry

    stats[...] = jnp.zeros_like(stats)
    lax.fori_loop(0, UNITS, body, 0)


def key_kernel(pos, mask, tab, stats, *refs):
    parts, kv = refs[:11], refs[11]
    m_ref, x_ref, pool, sems = refs[12:]
    fetch(parts, pool, sems)
    zh, p = pos[0], pos[1]

    def body(unit, carry):
        is_x = unit == 4
        z = jnp.where(is_x, zh, unit)
        own = jnp.where(is_x, 0, unit + 1)
        k = rows_of(kv, own, 0)
        v = rows_of(kv, own, 1)
        dk = jnp.zeros((TOK, E), F32)
        dv = jnp.zeros((TOK, E), F32)
        for offset in OFFSETS:
            group, other, valid, slot = source(offset, unit, zh, p)
            at = jnp.where(is_x, other, zh * PLANE + lax.rem(other, PLANE))
            row = 2 * jnp.where(is_x, 4, lax.div(other, PLANE))
            total = stats[at, pl.ds(row, 1), :]
            delta = stats[at, pl.ds(row + 1, 1), :]
            q = rows_of(pool, slot, 0)
            g = rows_of(pool, slot, 1)
            st = add_bias(dot(k, q, 1, 1), bias_of(mask, other, group, valid))
            w = jnp.exp2(st * COEF - total)
            ds = (w * (dot(v, g, 1, 1) - delta)).astype(BF16)
            dv = dv + dot(w.astype(BF16), g, 1, 0)
            dk = dk + dot(ds, q, 1, 0)
        put(unit, m_ref, x_ref, 0, unturn(dk * SCALE, tab, z).astype(BF16))
        put(unit, m_ref, x_ref, 1, dv.astype(BF16))
        return carry

    lax.fori_loop(0, UNITS, body, 0)


M_OUT = jax.ShapeDtypeStruct((16, 2, QTR, E), BF16)
X_OUT = jax.ShapeDtypeStruct((4, 2, QTR, E), BF16)


def query_side(pos, mask, tab, parts, qg):
    return pl.pallas_call(
        query_kernel,
        out_shape=(M_OUT, X_OUT, jax.ShapeDtypeStruct((16, TOK), F32)),
        in_specs=[SMEM, SMEM, VMEM] + [ANY] * 11 + [VMEM],
        out_specs=(VMEM, VMEM, VMEM),
        scratch_shapes=[
            pltpu.VMEM((SLOTS, 4, 2, QTR, E), BF16),
            pltpu.SemaphoreType.DMA((11,)),
            pltpu.VMEM((len(OFFSETS), TOK, TOK), F32),
        ],
        compiler_params=pltpu.CompilerParams(vmem_limit_bytes=40 * 2**20),
        cost_estimate=pl.CostEstimate(
            flops=65 * 5 * 2 * TOK * TOK * E, bytes_accessed=8 * 2**20, transcendentals=65 * TOK * TOK
        ),
        name="query_side",
    )(pos, mask, tab, *parts, qg)


def key_side(pos, mask, tab, stats, parts, kv):
    return pl.pallas_call(
        key_kernel,
        out_shape=(M_OUT, X_OUT),
        in_specs=[SMEM, SMEM, VMEM, VMEM] + [ANY] * 11 + [VMEM],
        out_specs=(VMEM, VMEM),
        scratch_shapes=[
            pltpu.VMEM((SLOTS, 4, 2, QTR, E), BF16),
            pltpu.SemaphoreType.DMA((11,)),
        ],
        compiler_params=pltpu.CompilerParams(vmem_limit_bytes=40 * 2**20),
        cost_estimate=pl.CostEstimate(
            flops=65 * 4 * 2 * TOK * TOK * E, bytes_accessed=8 * 2**20, transcendentals=65 * TOK * TOK
        ),
        name="key_side",
    )(pos, mask, tab, stats, *parts, kv)


def tables(block_frame, p):
    inv = np.zeros((E,), np.float32)
    inv[:HALF] = 10000.0 ** (-2.0 * np.arange(HALF, dtype=np.float32) / ROT)
    inv[HALF:ROT] = inv[:HALF]
    first = (np.arange(E) < HALF).astype(np.float32)
    second = ((np.arange(E) >= HALF) & (np.arange(E) < ROT)).astype(np.float32)
    frames = block_frame.reshape(ZG, PLANE, 2)
    frames = lax.dynamic_slice(frames, (0, p, 0), (ZG, 1, 2)).reshape(2 * ZG)
    angles = frames.astype(F32)[:, None] * inv[None]
    sine = jnp.sin(angles)
    zero = jnp.zeros_like(sine)
    return jnp.stack(
        [jnp.cos(angles), sine * second, -sine * first, zero, zero, zero, zero, zero], axis=1
    )


def spread(m, x, p):
    m = lax.all_to_all(m, ("zh", "h"), 0, 0, tiled=True).reshape(4, 4, 2, QTR, E)
    x = lax.all_to_all(x, "h", 0, 0, tiled=True).reshape(1, 4, 2, QTR, E)
    above = lax.ppermute(x, "zh", [(0, 1), (1, 2), (2, 3)])
    below = lax.ppermute(x, "zh", [(1, 0), (2, 1), (3, 2)])
    across = lax.ppermute(x, "zh", [(0, 2), (2, 0), (1, 3), (3, 1)])
    last = jnp.where(p < 8, below, above)
    own = jnp.concatenate([x, m, last], axis=0)
    parts = []
    for s in SHIFTS:
        if s == 8:
            message = own
        else:
            wraps = (p + s < 0) | (p + s >= PLANE)
            message = lax.dynamic_slice_in_dim(own, jnp.where(wraps, 1, 0), 5, axis=0)
        parts.append(lax.ppermute(message, "p", [(i, (i + s) % PLANE) for i in range(PLANE)]))
    return own, parts + [own, above, below, across]


def leave(m, x):
    m = lax.all_to_all(m, ("zh", "h"), 0, 0, tiled=True)
    x = lax.all_to_all(x, "h", 0, 0, tiled=True)
    return unpack(m, x)


def shards(queries, key_vectors, value_vectors, grad_output, block_mask, block_frame):
    zh, p, h = lax.axis_index("zh"), lax.axis_index("p"), lax.axis_index("h")
    pos = jnp.stack([zh, p, h]).astype(jnp.int32)
    tab = tables(block_frame, p)
    km, kx = pack(pos, tab, key_vectors, value_vectors)
    qm, qx = pack(pos, tab, queries, grad_output)
    kv, kv_parts = spread(km, kx, p)
    qg, qg_parts = spread(qm, qx, p)
    am, ax, stats = query_side(pos, block_mask, tab, kv_parts, qg)
    stats = lax.all_gather(stats, ("zh", "p"), axis=0, tiled=False)
    bm, bx = key_side(pos, block_mask, tab, stats, qg_parts, kv)
    attended, grad_q = leave(am, ax)
    grad_k, grad_v = leave(bm, bx)
    return attended, grad_q, grad_k, grad_v


def solution(mesh):
    fine = Mesh(mesh.devices.reshape(ZG, PLANE, 4), ("zh", "p", "h"))
    tok = P(("zh", "p", "h"), None, None)
    return jax.shard_map(
        shards,
        mesh=fine,
        in_specs=(tok, tok, tok, tok, P(), P()),
        out_specs=(tok, tok, tok, tok),
        check_vma=False,
    )
```

```python
import functools
import math

import jax
import jax.numpy as jnp
import numpy as np
from jax import lax
from jax.experimental import pallas as pl
from jax.experimental.pallas import tpu as pltpu
from jax.sharding import Mesh, PartitionSpec as P

ROT = 44
HALF = ROT // 2
BLK = 128
E = 128
TOK = 256
QTR = 64
GROUPS = 64
PLANE = 16
ZG = 4
UNITS = 5
NEG = -1e30
PARTS = 8
BASES = (0, 6, 12, 18, 24, 30, 36, 41)
OFFSETS = (0, 1, -1, 2, -2, 4, -4, 8, -8, 16, -16, 32, -32)
SLOTS = 46
SCALE = 1.0 / math.sqrt(E)
LOG2E = 1.4426950408889634
COEF = SCALE * LOG2E
F32 = jnp.float32
BF16 = jnp.bfloat16
ANY = pl.BlockSpec(memory_space=pl.ANY)
SMEM = pl.BlockSpec(memory_space=pltpu.SMEM)
VMEM = pl.BlockSpec(memory_space=pltpu.VMEM)

M_OUT = jax.ShapeDtypeStruct((16, 2, QTR, E), BF16)
X_OUT = jax.ShapeDtypeStruct((4, 2, QTR, E), BF16)
WIDE = jax.ShapeDtypeStruct((16, 2, 2, QTR, E), BF16)
SUMS = jax.ShapeDtypeStruct((UNITS, 2, TOK, E), F32)


def dot(a, b, ca, cb):
    return lax.dot_general(a, b, (((ca,), (cb,)), ((), ())), preferred_element_type=F32)


def turn(x, c, s1, s2):
    return x * c + pltpu.roll(x, HALF, x.ndim - 1) * s1 + pltpu.roll(x, E - HALF, x.ndim - 1) * s2


def pack_kernel(pos, tab, a_ref, b_ref, o_ref):
    t = tab[2 * pos[0] + pos[2] // 2]
    a = turn(a_ref[...].astype(F32), t[0:1][None], t[1:2][None], t[2:3][None]).astype(BF16)
    for n, val in ((0, a), (1, b_ref[...])):
        o_ref[:, 0, n] = val[:16]
        for i in range(4):
            o_ref[4 * i : 4 * i + 4, 1, n] = val[16:]


def pack(pos, tab, *tensors):
    return pl.pallas_call(
        pack_kernel,
        out_shape=WIDE,
        in_specs=[SMEM, VMEM, VMEM, VMEM],
        out_specs=VMEM,
        compiler_params=pltpu.CompilerParams(vmem_limit_bytes=40 * 2**20),
        name="pack",
    )(pos, tab, *[jnp.transpose(t, (1, 0, 2)) for t in tensors])


def unpack_kernel(m_ref, x_ref, a_ref, b_ref):
    for i, o in ((0, a_ref), (1, b_ref)):
        o[:16] = m_ref[:, i]
        o[16:] = x_ref[:, i]


def unpack(m, x):
    shape = jax.ShapeDtypeStruct((20, QTR, E), BF16)
    a, b = pl.pallas_call(
        unpack_kernel,
        out_shape=(shape, shape),
        in_specs=[VMEM, VMEM],
        out_specs=(VMEM, VMEM),
        compiler_params=pltpu.CompilerParams(vmem_limit_bytes=40 * 2**20),
        name="unpack",
    )(m, x)
    return jnp.transpose(a, (1, 0, 2)), jnp.transpose(b, (1, 0, 2))


def source(offset, unit, zh, p):
    is_x = unit == 4
    z = jnp.where(is_x, zh, unit)
    group = z * PLANE + p
    other = group - offset
    valid = (other >= 0) & (other < GROUPS)
    if local(offset):
        slot = jnp.clip(z - offset // PLANE, 0, ZG - 1)
    else:
        x = lax.rem(p, 4)
        up, down, eight, across, first, second, left, right = BASES
        base = {
            4: lambda: up,
            -4: lambda: down,
            8: lambda: eight,
            -8: lambda: eight,
            1: lambda: jnp.where(x == 0, first, left),
            -1: lambda: jnp.where(x == 3, first, right),
            2: lambda: jnp.where(x == 0, second, jnp.where(x == 1, first, across)),
            -2: lambda: jnp.where(x == 3, second, jnp.where(x == 2, first, across)),
        }[offset]()
        at = p - offset
        step = jnp.where(at < 0, -1, jnp.where(at >= PLANE, 1, 0))
        zz = jnp.clip(z + step, 0, ZG - 1)
        slot = base + jnp.where(is_x, 5 * step * step, 1 + zz)
    return group, jnp.clip(other, 0, GROUPS - 1), valid, slot


def local(offset):
    return offset == 0 or abs(offset) >= PLANE


def add_bias(st, bias):
    top = jnp.concatenate([st[:BLK, :BLK] + bias[0][0], st[:BLK, BLK:] + bias[0][1]], axis=1)
    low = jnp.concatenate([st[BLK:, :BLK] + bias[1][0], st[BLK:, BLK:] + bias[1][1]], axis=1)
    return jnp.concatenate([top, low], axis=0)


def bias_of(mask, q_group, k_group, valid):
    return [
        [
            jnp.where(valid & (mask[2 * q_group + qb, 2 * k_group + kb] != 0), 0.0, NEG)
            for qb in range(2)
        ]
        for kb in range(2)
    ]


def fetch(parts, pool, sems, first):
    at = 0
    copies = []
    for n, ref in enumerate(parts):
        copy = pltpu.make_async_copy(ref, pool.at[pl.ds(at, ref.shape[0])], sems.at[first + n])
        copy.start()
        copies.append(copy)
        at += ref.shape[0]
    return copies


def near(ref, z, unit, which):
    return ref[z, :, jnp.where(unit == 4, 1, 0), which].reshape(TOK, E)


def far(ref, slot, which):
    return ref[slot, :, which].reshape(TOK, E)


def unturn(x, tab, z):
    halves = []
    for blk in range(2):
        t = tab[2 * z + blk]
        halves.append(turn(x[blk * BLK : (blk + 1) * BLK], t[0:1], -t[1:2], -t[2:3]))
    return jnp.concatenate(halves, axis=0)


def put(unit, m_ref, x_ref, which, val):
    for b in range(4):
        piece = val[b * QTR : (b + 1) * QTR]

        @pl.when(unit < 4)
        def _():
            m_ref[unit * 4 + b, which] = piece

        @pl.when(unit == 4)
        def _():
            x_ref[b, which] = piece


def query_kernel(pos, mask, tab, kv, qg, *refs):
    parts = refs[:PARTS]
    m_ref, x_ref, stats, pool, sems, scores = refs[PARTS:]
    copies = fetch(parts, pool, sems, 0)
    for copy in copies:
        copy.wait()
    zh, p = pos[0], pos[1]

    def body(unit, carry):
        z = jnp.where(unit == 4, zh, unit)
        q = near(qg, z, unit, 0)
        g = near(qg, z, unit, 1)
        gt = jnp.transpose(g.astype(F32))
        slots = []
        top = jnp.full((1, TOK), NEG, F32)

        def take(n, which):
            if local(OFFSETS[n]):
                return near(kv, slots[n], unit, which)
            return far(pool, slots[n], which)

        for n, offset in enumerate(OFFSETS):
            group, other, valid, slot = source(offset, unit, zh, p)
            slots.append(slot)
            st = add_bias(dot(take(n, 0), q, 1, 1), bias_of(mask, group, other, valid))
            scores[n] = st
            top = jnp.maximum(top, jnp.max(st, axis=0, keepdims=True))
        top = top * COEF
        total = jnp.zeros((1, TOK), F32)
        out = jnp.zeros((E, TOK), F32)
        for n in range(len(OFFSETS)):
            w = jnp.exp2(scores[n] * COEF - top)
            scores[n] = w
            total = total + jnp.sum(w, axis=0, keepdims=True)
            out = out + dot(take(n, 1), w.astype(BF16), 0, 0)
        inv = 1.0 / total
        att = (out * inv).astype(BF16)
        delta = jnp.sum(gt * att.astype(F32), axis=0, keepdims=True)
        stats[pl.ds(2 * unit, 1), :] = top + jnp.log2(total)
        stats[pl.ds(2 * unit + 1, 1), :] = delta
        dq = jnp.zeros((E, TOK), F32)
        for n in range(len(OFFSETS)):
            dp = dot(take(n, 1), g, 1, 1)
            ds = (scores[n] * inv * (dp - delta)).astype(BF16)
            dq = dq + dot(take(n, 0), ds, 0, 0)
        put(unit, m_ref, x_ref, 0, jnp.transpose(att.astype(F32)).astype(BF16))
        put(unit, m_ref, x_ref, 1, unturn(jnp.transpose(dq * SCALE), tab, z).astype(BF16))
        return carry

    stats[...] = jnp.zeros_like(stats)
    lax.fori_loop(0, UNITS, body, 0)


def key_terms(offsets, zh, p, mask, unit, kv, take, dk, dv):
    is_x = unit == 4
    z = jnp.where(is_x, zh, unit)
    k = near(kv, z, unit, 0)
    v = near(kv, z, unit, 1)
    for offset in offsets:
        group, other, valid, slot = source(offset, unit, zh, p)
        row = 2 * (lax.div(other, PLANE) + jnp.where(is_x, ZG, 0))
        q, g, total, delta = take(offset, slot, lax.rem(other, PLANE), row)
        st = add_bias(dot(k, q, 1, 1), bias_of(mask, other, group, valid))
        w = jnp.exp2(st * COEF - total)
        ds = (w * (dot(v, g, 1, 1) - delta)).astype(BF16)
        dv = dv + dot(w.astype(BF16), g, 1, 0)
        dk = dk + dot(ds, q, 1, 0)
    return dk, dv


def near_key_kernel(pos, mask, kv, qg, stats, sums):
    zh, p = pos[0], pos[1]

    def body(unit, carry):
        def take(offset, z, at, row):
            total = stats[pl.ds(row, 1), :]
            return near(qg, z, unit, 0), near(qg, z, unit, 1), total, stats[pl.ds(row + 1, 1), :]

        zero = jnp.zeros((TOK, E), F32)
        offsets = [o for o in OFFSETS if local(o)]
        dk, dv = key_terms(offsets, zh, p, mask, unit, kv, take, zero, zero)
        sums[unit, 0] = dk
        sums[unit, 1] = dv
        return carry

    lax.fori_loop(0, UNITS, body, 0)


def far_key_kernel(pos, mask, tab, kv, sums, stats, *refs):
    m_ref, x_ref, pool, sems = refs[PARTS:]
    for copy in fetch(refs[:PARTS], pool, sems, 0):
        copy.wait()
    zh, p = pos[0], pos[1]

    def body(unit, carry):
        def take(offset, slot, at, row):
            total = stats[at, pl.ds(row, 1), :]
            return far(pool, slot, 0), far(pool, slot, 1), total, stats[at, pl.ds(row + 1, 1), :]

        offsets = [o for o in OFFSETS if not local(o)]
        dk, dv = key_terms(
            offsets, zh, p, mask, unit, kv, take, sums[unit, 0], sums[unit, 1]
        )
        z = jnp.where(unit == 4, zh, unit)
        put(unit, m_ref, x_ref, 0, unturn(dk * SCALE, tab, z).astype(BF16))
        put(unit, m_ref, x_ref, 1, dv.astype(BF16))
        return carry

    lax.fori_loop(0, UNITS, body, 0)


def cost(pairs, products):
    return pl.CostEstimate(
        flops=pairs * products * 2 * TOK * TOK * E,
        bytes_accessed=8 * 2**20,
        transcendentals=pairs * TOK * TOK,
    )


LIMIT = pltpu.CompilerParams(vmem_limit_bytes=40 * 2**20)


def query_side(pos, mask, tab, kv, qg, parts):
    return pl.pallas_call(
        query_kernel,
        out_shape=(M_OUT, X_OUT, jax.ShapeDtypeStruct((16, TOK), F32)),
        in_specs=[SMEM, SMEM, VMEM, VMEM, VMEM] + [ANY] * PARTS,
        out_specs=(VMEM, VMEM, VMEM),
        scratch_shapes=[
            pltpu.VMEM((SLOTS, 4, 2, QTR, E), BF16),
            pltpu.SemaphoreType.DMA((PARTS,)),
            pltpu.VMEM((len(OFFSETS), TOK, TOK), F32),
        ],
        compiler_params=LIMIT,
        cost_estimate=cost(65, 5),
        name="query_side",
    )(pos, mask, tab, kv, qg, *parts)


def near_key_side(pos, mask, kv, qg, stats):
    return pl.pallas_call(
        near_key_kernel,
        out_shape=SUMS,
        in_specs=[SMEM, SMEM, VMEM, VMEM, VMEM],
        out_specs=VMEM,
        compiler_params=LIMIT,
        cost_estimate=cost(25, 4),
        name="near_key_side",
    )(pos, mask, kv, qg, stats)


def far_key_side(pos, mask, tab, kv, sums, stats, parts):
    return pl.pallas_call(
        far_key_kernel,
        out_shape=(M_OUT, X_OUT),
        in_specs=[SMEM, SMEM, VMEM, VMEM, VMEM, VMEM] + [ANY] * PARTS,
        out_specs=(VMEM, VMEM),
        scratch_shapes=[
            pltpu.VMEM((SLOTS, 4, 2, QTR, E), BF16),
            pltpu.SemaphoreType.DMA((PARTS,)),
        ],
        compiler_params=LIMIT,
        cost_estimate=cost(40, 4),
        name="far_key_side",
    )(pos, mask, tab, kv, sums, stats, *parts)


def tables(block_frame, p):
    inv = np.zeros((E,), np.float32)
    inv[:HALF] = 10000.0 ** (-2.0 * np.arange(HALF, dtype=np.float32) / ROT)
    inv[HALF:ROT] = inv[:HALF]
    first = (np.arange(E) < HALF).astype(np.float32)
    second = ((np.arange(E) >= HALF) & (np.arange(E) < ROT)).astype(np.float32)
    frames = block_frame.reshape(ZG, PLANE, 2)
    frames = lax.dynamic_slice(frames, (0, p, 0), (ZG, 1, 2)).reshape(2 * ZG)
    angles = frames.astype(F32)[:, None] * inv[None]
    sine = jnp.sin(angles)
    zero = jnp.zeros_like(sine)
    return jnp.stack(
        [jnp.cos(angles), sine * second, -sine * first, zero, zero, zero, zero, zero], axis=1
    )


def move(value, rule):
    pairs = []
    for y in range(4):
        for x in range(4):
            to = rule(x, y)
            if to is not None:
                pairs.append((4 * y + x, 4 * (to[1] % 4) + to[0] % 4))
    return lax.ppermute(value, "p", pairs)


def start_exchange(own):
    across = move(own, lambda x, y: (x + 2, y))
    up = move(own, lambda x, y: (x, y + 1))
    down = move(own, lambda x, y: (x, y - 1))
    left = move(own[:5], lambda x, y: (x + 1, y) if x < 3 else None)
    right = move(own[:5], lambda x, y: (x - 1, y) if x > 0 else None)
    return up, down, across, left, right


def end_exchange(up, down, across, left, right, p):
    x = lax.rem(p, 4)
    turned = jnp.where(x < 2, down, up)
    eight = move(turned, lambda x, y: (x, y - 1) if x < 2 else (x, y + 1))
    first = move(
        jnp.where((x == 0) | (x == 3), turned, across),
        lambda x, y: ((3, y), (1, y + 1), (2, y - 1), (0, y))[x],
    )
    second = move(across, lambda x, y: ((0, y + 1), None, None, (3, y - 1))[x])
    return up, down, eight, across, first, second, left, right


def slots_of(m, x, zh, p):
    first = lax.dynamic_slice_in_dim(x, zh, 1, axis=0)
    wrap = jnp.clip(zh + jnp.where(p < 8, 1, -1), 0, ZG - 1)
    return jnp.concatenate([first, m, lax.dynamic_slice_in_dim(x, wrap, 1, axis=0)], axis=0)


def gather_heads(packed):
    wide = lax.all_to_all(packed, ("zh", "h"), 0, 0, tiled=True)
    return wide.reshape(4, 4, 2, 2, QTR, E)


def leave(m, x):
    m = lax.all_to_all(m, ("zh", "h"), 0, 0, tiled=True)
    x = lax.all_to_all(x, "h", 0, 0, tiled=True)
    return unpack(m, x)


def shards(queries, key_vectors, value_vectors, grad_output, block_mask, block_frame):
    zh, p, h = lax.axis_index("zh"), lax.axis_index("p"), lax.axis_index("h")
    pos = jnp.stack([zh, p, h]).astype(jnp.int32)
    tab = tables(block_frame, p)
    kv = gather_heads(pack(pos, tab, key_vectors, value_vectors))
    qg = gather_heads(pack(pos, tab, queries, grad_output))
    kv_first = start_exchange(slots_of(kv[:, :, 0], kv[:, :, 1], zh, p))
    kv_parts = end_exchange(*kv_first, p)
    qg_own = slots_of(qg[:, :, 0], qg[:, :, 1], zh, p)
    qg_own, kv_some = lax.optimization_barrier((qg_own, kv_first[:3]))
    qg_first = start_exchange(qg_own)
    am, ax, stats = query_side(pos, block_mask, tab, kv, qg, kv_parts)
    xs = jnp.broadcast_to(stats[None, 8:10], (4, 2, TOK))
    xs = lax.all_to_all(xs, "zh", 0, 0, tiled=True).reshape(8, TOK)
    stats = jnp.concatenate([stats[:8], xs], axis=0)
    every = lax.all_to_all(
        jnp.broadcast_to(stats[None], (PLANE, 16, TOK)), "p", 0, 0, tiled=True
    )
    qg_first, am = lax.optimization_barrier((qg_first, am))
    qg_parts = end_exchange(*qg_first, p)
    sums = near_key_side(pos, block_mask, kv, qg, stats)
    attended, grad_q = leave(am, ax)
    sums, attended, grad_q = lax.optimization_barrier((sums, attended, grad_q))
    bm, bx = far_key_side(pos, block_mask, tab, kv, sums, every, qg_parts)
    grad_k, grad_v = leave(bm, bx)
    return attended, grad_q, grad_k, grad_v


def solution(mesh):
    fine = Mesh(mesh.devices.reshape(ZG, PLANE, 4), ("zh", "p", "h"))
    tok = P(("zh", "p", "h"), None, None)
    return jax.shard_map(
        shards,
        mesh=fine,
        in_specs=(tok, tok, tok, tok, P(), P()),
        out_specs=(tok, tok, tok, tok),
        check_vma=False,
    )
```

```python
import functools
import math

import jax
import jax.numpy as jnp
import numpy as np
from jax import lax
from jax.experimental import pallas as pl
from jax.experimental.pallas import tpu as pltpu
from jax.sharding import Mesh, PartitionSpec as P

ROT = 44
HALF = ROT // 2
BLK = 128
E = 128
TOK = 256
QTR = 64
GROUPS = 64
PLANE = 16
ZG = 4
UNITS = 5
SROWS = 24
NEG = -1e30
PARTS = 8
OFFSETS = (0, 1, -1, 2, -2, 4, -4, 8, -8, 16, -16, 32, -32)
SLOTS = 46
SCALE = 1.0 / math.sqrt(E)
LOG2E = 1.4426950408889634
COEF = SCALE * LOG2E
F32 = jnp.float32
BF16 = jnp.bfloat16
HBM = pl.BlockSpec(memory_space=pltpu.HBM)
SMEM = pl.BlockSpec(memory_space=pltpu.SMEM)
VMEM = pl.BlockSpec(memory_space=pltpu.VMEM)

WIDE = jax.ShapeDtypeStruct((16, 2, 2, QTR, E), BF16)


def dot(a, b, ca, cb):
    return lax.dot_general(a, b, (((ca,), (cb,)), ((), ())), preferred_element_type=F32)


def turn(x, c, s1, s2):
    return x * c + pltpu.roll(x, HALF, x.ndim - 1) * s1 + pltpu.roll(x, E - HALF, x.ndim - 1) * s2


def pack_kernel(pos, frames, rates, a_hbm, b_hbm, o_ref, a_ref, b_ref, sems):
    copies = [
        pltpu.make_async_copy(a_hbm, a_ref, sems.at[0]),
        pltpu.make_async_copy(b_hbm, b_ref, sems.at[1]),
    ]
    for copy in copies:
        copy.start()
    block = 2 * (pos[0] * PLANE + pos[1]) + pos[2] // 2
    rows = [r[None] for r in turn_rows(frames, rates, block)]
    copies[0].wait()
    a = turn(a_ref[...].astype(F32), *rows).astype(BF16)
    copies[1].wait()
    for n, val in ((0, a), (1, b_ref[...])):
        o_ref[:, 0, n] = val[:16]
        for i in range(4):
            o_ref[4 * i : 4 * i + 4, 1, n] = val[16:]


def pack(pos, frames, rates, *tensors):
    return pl.pallas_call(
        pack_kernel,
        out_shape=WIDE,
        in_specs=[SMEM, SMEM, VMEM, HBM, HBM],
        out_specs=VMEM,
        scratch_shapes=[
            pltpu.VMEM((20, QTR, E), BF16),
            pltpu.VMEM((20, QTR, E), BF16),
            pltpu.SemaphoreType.DMA((2,)),
        ],
        compiler_params=LIMIT,
        name="pack",
    )(pos, frames, rates, *[jnp.transpose(t, (1, 0, 2)) for t in tensors])


def unpack_kernel(pos, a_ref, b_ref, *refs):
    pieces, outs = refs[:4], refs[4:]
    for i, o in enumerate(outs):
        o[:16] = (a_ref, b_ref)[i // 2][:, i % 2]
        for n, piece in enumerate(pieces):
            o[16 + lax.rem(pos[2] - n + 4, 4)] = piece[i]


def unpack(pos, a, b, pieces):
    shape = jax.ShapeDtypeStruct((20, QTR, E), BF16)
    outs = pl.pallas_call(
        unpack_kernel,
        out_shape=(shape,) * 4,
        in_specs=[SMEM] + [VMEM] * 6,
        out_specs=(VMEM,) * 4,
        compiler_params=LIMIT,
        name="unpack",
    )(pos, a, b, *pieces)
    return tuple(jnp.transpose(o, (1, 0, 2)) for o in outs)


def source(offset, unit, zh, p):
    is_x = unit == 4
    z = jnp.where(is_x, zh, unit)
    group = z * PLANE + p
    other = group - offset
    valid = (other >= 0) & (other < GROUPS)
    if local(offset):
        slot = jnp.clip(z - offset // PLANE, 0, ZG - 1)
    else:
        x = lax.rem(p, 4)
        low = x < 2
        base = {
            4: lambda: 0,
            -4: lambda: 6,
            8: lambda: 12,
            -8: lambda: 12,
            1: lambda: jnp.where(x == 0, 30, 36),
            -1: lambda: jnp.where(x == 3, 30, 41),
            2: lambda: jnp.where(low, 24, 18),
            -2: lambda: jnp.where(low, 18, 24),
        }[offset]()
        at = p - offset
        step = jnp.where(at < 0, -1, jnp.where(at >= PLANE, 1, 0))
        zz = jnp.clip(z + step, 0, ZG - 1)
        slot = base + jnp.where(is_x, 5 * step * step, 1 + zz)
    return group, jnp.clip(other, 0, GROUPS - 1), valid, slot


def local(offset):
    return offset == 0 or abs(offset) >= PLANE


def add_bias(st, bias):
    top = jnp.concatenate([st[:BLK, :BLK] + bias[0][0], st[:BLK, BLK:] + bias[0][1]], axis=1)
    low = jnp.concatenate([st[BLK:, :BLK] + bias[1][0], st[BLK:, BLK:] + bias[1][1]], axis=1)
    return jnp.concatenate([top, low], axis=0)


def bias_of(mask, q_group, k_group, valid):
    return [
        [
            jnp.where(valid & (mask[2 * q_group + qb, 2 * k_group + kb] != 0), 0.0, NEG)
            for qb in range(2)
        ]
        for kb in range(2)
    ]


def fetch(parts, pool, sems, wholes=(), only_x=False):
    copies = []
    at = 0
    for n, ref in enumerate(parts):
        size = ref.shape[0]
        for first, count in (((0, 1), (5, 1)) if only_x else ((0, size),)):
            if first < size:
                copies.append(
                    pltpu.make_async_copy(
                        ref.at[pl.ds(first, count)],
                        pool.at[pl.ds(at + first, count)],
                        sems.at[2 * n + (first > 0)],
                    )
                )
        at += size
    for n, (whole, target) in enumerate(wholes):
        copies.append(pltpu.make_async_copy(whole, target, sems.at[2 * PARTS + n]))
    for copy in copies:
        copy.start()
    for copy in copies:
        copy.wait()


def near(ref, z, unit, which):
    return ref[z, :, jnp.where(unit == 4, 1, 0), which].reshape(TOK, E)


def far(ref, slot, which):
    return ref[slot, :, which].reshape(TOK, E)


def turn_rows(frames, rates, block):
    angles = frames[block].astype(F32) * rates[0:1]
    sine = jnp.sin(angles)
    return jnp.cos(angles), sine * rates[1:2], sine * rates[2:3]


def unturn(x, frames, rates, group):
    halves = []
    for blk in range(2):
        c, s1, s2 = turn_rows(frames, rates, 2 * group + blk)
        halves.append(turn(x[blk * BLK : (blk + 1) * BLK], c, -s1, -s2))
    return jnp.concatenate(halves, axis=0)


def put(ref, at, which, val):
    for b in range(4):
        ref[at, b, which] = val[b * QTR : (b + 1) * QTR]


def read_stats(ref, unit, *at):
    rows = [ref[(*at, pl.ds(4 * unit + n, 1), slice(None))] for n in range(4)]
    return jnp.concatenate(rows[:2], axis=1), jnp.concatenate(rows[2:], axis=1)


def pool_rows(offset, slot, unit, near_ref, pool, which):
    if local(offset):
        return near(near_ref, slot, unit, which)
    return far(pool, slot, which)


def forward_kernel(pos, *refs):
    parts, wholes, rest = refs[:PARTS], refs[PARTS : PARTS + 3], refs[PARTS + 3 :]
    att_ref, stats, pool, sems, mask, kv, qg, scores = rest
    fetch(parts, pool, sems, zip(wholes, (mask, kv, qg)))
    zh, p = pos[0], pos[1]

    def body(unit, carry):
        z = jnp.where(unit == 4, zh, unit)
        q = near(qg, z, unit, 0)
        slots = []
        top = jnp.full((1, TOK), NEG, F32)
        for n, offset in enumerate(OFFSETS):
            group, other, valid, slot = source(offset, unit, zh, p)
            slots.append(slot)
            k = pool_rows(offset, slot, unit, kv, pool, 0)
            st = add_bias(dot(k, q, 1, 1), bias_of(mask, group, other, valid))
            scores[n] = st
            top = jnp.maximum(top, jnp.max(st, axis=0, keepdims=True))
        top = top * COEF
        total = jnp.zeros((1, TOK), F32)
        out = jnp.zeros((E, TOK), F32)
        for n, offset in enumerate(OFFSETS):
            w = jnp.exp2(scores[n] * COEF - top)
            total = total + jnp.sum(w, axis=0, keepdims=True)
            v = pool_rows(offset, slots[n], unit, kv, pool, 1)
            out = out + dot(v, w.astype(BF16), 0, 0)
        att = jnp.transpose(out * (1.0 / total)).astype(BF16)
        put(att_ref, unit, 0, att)
        g = near(qg, z, unit, 1).astype(F32)
        delta = jnp.sum(jnp.transpose(g * att.astype(F32)), axis=0, keepdims=True)
        for n, row in enumerate((top + jnp.log2(total), delta)):
            stats[pl.ds(4 * unit + 2 * n, 1), :] = row[:, :BLK]
            stats[pl.ds(4 * unit + 2 * n + 1, 1), :] = row[:, BLK:]
        return carry

    stats[...] = jnp.zeros_like(stats)
    lax.fori_loop(0, UNITS, body, 0)


def query_kernel(pos, frames, rates, *refs):
    parts, wholes, rest = refs[:PARTS], refs[PARTS : PARTS + 5], refs[PARTS + 5 :]
    o_ref, pool, sems, mask, kv, qg, att, stats = rest
    fetch(parts, pool, sems, zip(wholes, (mask, kv, qg, att, stats)))
    zh, p = pos[0], pos[1]

    def body(unit, carry):
        z = jnp.where(unit == 4, zh, unit)
        q = near(qg, z, unit, 0)
        g = near(qg, z, unit, 1)
        total, delta = read_stats(stats, unit)
        dq = jnp.zeros((E, TOK), F32)
        for offset in OFFSETS:
            group, other, valid, slot = source(offset, unit, zh, p)
            k = pool_rows(offset, slot, unit, kv, pool, 0)
            v = pool_rows(offset, slot, unit, kv, pool, 1)
            st = add_bias(dot(k, q, 1, 1), bias_of(mask, group, other, valid))
            w = jnp.exp2(st * COEF - total)
            ds = (w * (dot(v, g, 1, 1) - delta)).astype(BF16)
            dq = dq + dot(k, ds, 0, 0)
        o_ref[unit, :, 0] = att[unit, :, 0]
        dq = unturn(jnp.transpose(dq * SCALE), frames, rates, z * PLANE + p)
        put(o_ref, unit, 1, dq.astype(BF16))
        return carry

    lax.fori_loop(0, UNITS, body, 0)


def key_terms(unit, zh, p, mask, kv, qg, pool, stats_of):
    z = jnp.where(unit == 4, zh, unit)
    k = near(kv, z, unit, 0)
    v = near(kv, z, unit, 1)
    dk = jnp.zeros((TOK, E), F32)
    dv = jnp.zeros((TOK, E), F32)
    for offset in OFFSETS:
        group, other, valid, slot = source(offset, unit, zh, p)
        total, delta = stats_of(other)
        q = pool_rows(offset, slot, unit, qg, pool, 0)
        g = pool_rows(offset, slot, unit, qg, pool, 1)
        st = add_bias(dot(k, q, 1, 1), bias_of(mask, other, group, valid))
        w = jnp.exp2(st * COEF - total)
        ds = (w * (dot(v, g, 1, 1) - delta)).astype(BF16)
        dv = dv + dot(w.astype(BF16), g, 1, 0)
        dk = dk + dot(ds, q, 1, 0)
    return dk, dv


def key_kernel(pos, frames, rates, *refs):
    parts, wholes, rest = refs[:PARTS], refs[PARTS : PARTS + 4], refs[PARTS + 4 :]
    o_ref, pool, sems, mask, kv, qg, stats = rest
    fetch(parts, pool, sems, zip(wholes, (mask, kv, qg, stats)))
    zh, p = pos[0], pos[1]

    def stats_of(other):
        return read_stats(stats, lax.div(other, PLANE), zh * PLANE + lax.rem(other, PLANE))

    def body(unit, carry):
        dk, dv = key_terms(unit, zh, p, mask, kv, qg, pool, stats_of)
        dk = unturn(dk * SCALE, frames, rates, unit * PLANE + p)
        put(o_ref, unit, 0, dk.astype(BF16))
        put(o_ref, unit, 1, dv.astype(BF16))
        return carry

    lax.fori_loop(0, ZG, body, 0)


def extra_key_kernel(pos, frames, rates, *refs):
    parts, wholes, rest = refs[:PARTS], refs[PARTS : PARTS + 5], refs[PARTS + 5 :]
    o_ref, pool, sems, mask, kv, qg, stats, done = rest
    fetch(parts, pool, sems, zip(wholes, (mask, kv, qg, stats, done)), only_x=True)
    zh, p, h = pos[0], pos[1], pos[2]

    def stats_of(other):
        return read_stats(stats, 4, other)

    dk, dv = key_terms(jnp.int32(4), zh, p, mask, kv, qg, pool, stats_of)
    dk = unturn(dk * SCALE, frames, rates, zh * PLANE + p).astype(BF16)
    dv = dv.astype(BF16)
    for b in range(4):
        to = lax.rem(b - h + 4, 4)
        o_ref[to, 0] = done[b, 0]
        o_ref[to, 1] = done[b, 1]
        o_ref[to, 2] = dk[b * QTR : (b + 1) * QTR]
        o_ref[to, 3] = dv[b * QTR : (b + 1) * QTR]


def cost(pairs, products):
    return pl.CostEstimate(
        flops=pairs * products * 2 * TOK * TOK * E,
        bytes_accessed=8 * 2**20,
        transcendentals=pairs * TOK * TOK,
    )


LIMIT = pltpu.CompilerParams(vmem_limit_bytes=60 * 2**20)


POOL = [
    pltpu.VMEM((SLOTS, 4, 2, QTR, E), BF16),
    pltpu.SemaphoreType.DMA((2 * PARTS + 5,)),
    pltpu.SMEM((2 * GROUPS, 2 * GROUPS), jnp.int32),
    pltpu.VMEM((4, 4, 2, 2, QTR, E), BF16),
    pltpu.VMEM((4, 4, 2, 2, QTR, E), BF16),
]
EVERY = pltpu.VMEM((GROUPS, SROWS, E), F32)


def side(kernel, out_shape, scratch, pairs, products, scalars, arrays):
    outs = out_shape if isinstance(out_shape, tuple) else (out_shape,)
    specs = [SMEM, SMEM, VMEM][: len(scalars)]
    return pl.pallas_call(
        kernel,
        out_shape=out_shape,
        in_specs=specs + [HBM] * len(arrays),
        out_specs=(VMEM,) * len(outs) if isinstance(out_shape, tuple) else VMEM,
        scratch_shapes=POOL + scratch,
        compiler_params=LIMIT,
        cost_estimate=cost(pairs, products),
        name=kernel.__name__,
    )(*scalars, *arrays)


def blocks(units, tensors):
    return jax.ShapeDtypeStruct((units, 4, tensors, QTR, E), BF16)


def forward_side(pos, mask, kv, qg, parts):
    shapes = (blocks(UNITS, 1), jax.ShapeDtypeStruct((SROWS, E), F32))
    scratch = [pltpu.VMEM((len(OFFSETS), TOK, TOK), F32)]
    return side(forward_kernel, shapes, scratch, 65, 2, (pos,), (*parts, mask, kv, qg))


def query_side(scalars, mask, kv, qg, att, stats, parts):
    scratch = [pltpu.VMEM((UNITS, 4, 1, QTR, E), BF16), pltpu.VMEM((SROWS, E), F32)]
    arrays = (*parts, mask, kv, qg, att, stats)
    return side(query_kernel, blocks(UNITS, 2), scratch, 65, 3, scalars, arrays)


def key_side(scalars, mask, kv, qg, stats, parts):
    return side(
        key_kernel, blocks(ZG, 2), [EVERY], 52, 4, scalars, (*parts, mask, kv, qg, stats)
    )


def extra_key_side(scalars, mask, kv, qg, stats, done, parts):
    shape = jax.ShapeDtypeStruct((4, 4, QTR, E), BF16)
    scratch = [EVERY, pltpu.VMEM((4, 2, QTR, E), BF16)]
    arrays = (*parts, mask, kv, qg, stats, done)
    return side(extra_key_kernel, shape, scratch, 13, 4, scalars, arrays)


def turn_rates():
    rates = np.zeros((8, E), np.float32)
    rates[0, :HALF] = 10000.0 ** (-2.0 * np.arange(HALF, dtype=np.float32) / ROT)
    rates[0, HALF:ROT] = rates[0, :HALF]
    rates[1, HALF:ROT] = 1.0
    rates[2, :HALF] = -1.0
    return rates


def move(value, rule):
    pairs = []
    for y in range(4):
        for x in range(4):
            to = rule(x, y)
            if to is not None:
                pairs.append((4 * y + x, 4 * (to[1] % 4) + to[0] % 4))
    return lax.ppermute(value, "p", pairs)


def start_exchange(own):
    across = move(own, lambda x, y: (x + 2, y))
    up = move(own, lambda x, y: (x, y + 1))
    down = move(own, lambda x, y: (x, y - 1))
    return up, down, across


def end_exchange(own5, up, down, across, turned):
    eight = move(turned, lambda x, y: (x, y - 1) if x < 2 else (x, y + 1))
    aslant = move(across, lambda x, y: (x, y + 1) if x < 2 else (x, y - 1))
    wrap = move(turned, lambda x, y: (3 - x, y) if x in (0, 3) else None)
    left = move(own5, lambda x, y: (x + 1, y) if x < 3 else None)
    right = move(own5, lambda x, y: (x - 1, y) if x > 0 else None)
    return up, down, eight, across, aslant, wrap, left, right


def slots_of(m, x, zh, p):
    first = lax.dynamic_slice_in_dim(x, zh, 1, axis=0)
    wrap = jnp.clip(zh + jnp.where(p < 8, 1, -1), 0, ZG - 1)
    return jnp.concatenate([first, m, lax.dynamic_slice_in_dim(x, wrap, 1, axis=0)], axis=0)


def gather_heads(packed):
    wide = lax.all_to_all(packed, ("zh", "h"), 0, 0, tiled=True)
    return wide.reshape(4, 4, 2, 2, QTR, E)


def shards(queries, key_vectors, value_vectors, grad_output, block_mask, block_frame):
    zh, p, h = lax.axis_index("zh"), lax.axis_index("p"), lax.axis_index("h")
    pos = jnp.stack([zh, p, h]).astype(jnp.int32)
    rates = turn_rates()
    low = lax.rem(p, 4) < 2
    kv = gather_heads(pack(pos, block_frame, rates, key_vectors, value_vectors))
    qg = pack(pos, block_frame, rates, queries, grad_output)
    kv_own = slots_of(kv[:, :, 0], kv[:, :, 1], zh, p)
    up, down, across = start_exchange(kv_own)
    qg, up, down, across = lax.optimization_barrier((qg, up, down, across))
    kv_parts = end_exchange(kv_own[:5], up, down, across, jnp.where(low, down, up))
    qg = gather_heads(qg)
    qg_own = slots_of(qg[:, :, 0], qg[:, :, 1], zh, p)
    qg_own, kv_some = lax.optimization_barrier((qg_own, kv_parts[2:6]))
    kv_parts = kv_parts[:2] + tuple(kv_some) + kv_parts[6:]
    up, down, across = start_exchange(qg_own)
    att, stats = forward_side(pos, block_mask, kv, qg, kv_parts)
    turned = jnp.where(low, down, up)
    own5, turned, across, att, stats = lax.optimization_barrier(
        (qg_own[:5], turned, across, att, stats)
    )
    qg_parts = end_exchange(own5, up, down, across, turned)
    every = lax.all_to_all(
        jnp.broadcast_to(stats[None], (GROUPS, SROWS, E)), ("zh", "p"), 0, 0, tiled=True
    )
    scalars = (pos, block_frame, rates)
    am = query_side(scalars, block_mask, kv, qg, att, stats, kv_parts)
    am, every, qg_parts = lax.optimization_barrier((am, every, qg_parts))
    bm = key_side(scalars, block_mask, kv, qg, every, qg_parts)
    out = lax.all_to_all(am[:4].reshape(16, 2, QTR, E), ("zh", "h"), 0, 0, tiled=True)
    out, bm = lax.optimization_barrier((out, bm))
    x = extra_key_side(scalars, block_mask, kv, qg, every, am[4], qg_parts)
    pieces = [x[0]] + [
        lax.ppermute(x[n], "h", [(i, (i + n) % 4) for i in range(4)]) for n in range(1, 4)
    ]
    bm = lax.all_to_all(bm.reshape(16, 2, QTR, E), ("zh", "h"), 0, 0, tiled=True)
    return unpack(pos, out, bm, pieces)


def solution(mesh):
    fine = Mesh(mesh.devices.reshape(ZG, PLANE, 4), ("zh", "p", "h"))
    tok = P(("zh", "p", "h"), None, None)
    return jax.shard_map(
        shards,
        mesh=fine,
        in_specs=(tok, tok, tok, tok, P(), P()),
        out_specs=(tok, tok, tok, tok),
        check_vma=False,
    )
```

```python
import functools
import math

import jax
import jax.numpy as jnp
import numpy as np
from jax import lax
from jax.experimental import pallas as pl
from jax.experimental.pallas import tpu as pltpu
from jax.sharding import Mesh, PartitionSpec as P

ROT = 44
HALF = ROT // 2
BLK = 128
E = 128
TOK = 256
QTR = 64
GROUPS = 64
PLANE = 16
ZG = 4
UNITS = 5
SROWS = 24
NEG = -1e30
PARTS = 8
OFFSETS = (0, 16, -16, 32, -32, 4, -4, 8, -8, 1, -1, 2, -2)
FIRST_FAR = 4
SLOTS = 46
SCALE = 1.0 / math.sqrt(E)
LOG2E = 1.4426950408889634
COEF = SCALE * LOG2E
F32 = jnp.float32
BF16 = jnp.bfloat16
HBM = pl.BlockSpec(memory_space=pltpu.HBM)
SMEM = pl.BlockSpec(memory_space=pltpu.SMEM)
VMEM = pl.BlockSpec(memory_space=pltpu.VMEM)

WIDE = jax.ShapeDtypeStruct((16, 2, 2, QTR, E), BF16)


def dot(a, b, ca, cb):
    return lax.dot_general(a, b, (((ca,), (cb,)), ((), ())), preferred_element_type=F32)


def turn(x, c, s1, s2):
    return x * c + pltpu.roll(x, HALF, x.ndim - 1) * s1 + pltpu.roll(x, E - HALF, x.ndim - 1) * s2


def pack_kernel(pos, frames, rates, a_hbm, b_hbm, o_ref, a_ref, b_ref, sems):
    copies = [
        pltpu.make_async_copy(a_hbm, a_ref, sems.at[0]),
        pltpu.make_async_copy(b_hbm, b_ref, sems.at[1]),
    ]
    for copy in copies:
        copy.start()
    block = 2 * (pos[0] * PLANE + pos[1]) + pos[2] // 2
    rows = [r[None] for r in turn_rows(frames, rates, block)]
    copies[0].wait()
    a = turn(a_ref[...].astype(F32), *rows).astype(BF16)
    copies[1].wait()
    for n, val in ((0, a), (1, b_ref[...])):
        o_ref[:, 0, n] = val[:16]
        for i in range(4):
            o_ref[4 * i : 4 * i + 4, 1, n] = val[16:]


def pack(pos, frames, rates, *tensors):
    return pl.pallas_call(
        pack_kernel,
        out_shape=WIDE,
        in_specs=[SMEM, SMEM, VMEM, HBM, HBM],
        out_specs=VMEM,
        scratch_shapes=[
            pltpu.VMEM((20, QTR, E), BF16),
            pltpu.VMEM((20, QTR, E), BF16),
            pltpu.SemaphoreType.DMA((2,)),
        ],
        compiler_params=LIMIT,
        name="pack",
    )(pos, frames, rates, *[jnp.transpose(t, (1, 0, 2)) for t in tensors])


def unpack_kernel(pos, a_ref, b_ref, *refs):
    pieces, outs = refs[:4], refs[4:]
    for i, o in enumerate(outs):
        o[:16] = (a_ref, b_ref)[i // 2][:, i % 2]
        for n, piece in enumerate(pieces):
            o[16 + lax.rem(pos[2] - n + 4, 4)] = piece[i]


def unpack(pos, a, b, pieces):
    shape = jax.ShapeDtypeStruct((20, QTR, E), BF16)
    outs = pl.pallas_call(
        unpack_kernel,
        out_shape=(shape,) * 4,
        in_specs=[SMEM] + [VMEM] * 6,
        out_specs=(VMEM,) * 4,
        compiler_params=LIMIT,
        name="unpack",
    )(pos, a, b, *pieces)
    return tuple(jnp.transpose(o, (1, 0, 2)) for o in outs)


def source(offset, unit, zh, p):
    is_x = unit == 4
    z = jnp.where(is_x, zh, unit)
    group = z * PLANE + p
    other = group - offset
    valid = (other >= 0) & (other < GROUPS)
    if local(offset):
        slot = jnp.clip(z - offset // PLANE, 0, ZG - 1)
    else:
        x = lax.rem(p, 4)
        low = x < 2
        base = {
            4: lambda: 0,
            -4: lambda: 6,
            8: lambda: 12,
            -8: lambda: 12,
            1: lambda: jnp.where(x == 0, 30, 36),
            -1: lambda: jnp.where(x == 3, 30, 41),
            2: lambda: jnp.where(low, 24, 18),
            -2: lambda: jnp.where(low, 18, 24),
        }[offset]()
        at = p - offset
        step = jnp.where(at < 0, -1, jnp.where(at >= PLANE, 1, 0))
        zz = jnp.clip(z + step, 0, ZG - 1)
        slot = base + jnp.where(is_x, 5 * step * step, 1 + zz)
    return group, jnp.clip(other, 0, GROUPS - 1), valid, slot


def local(offset):
    return offset == 0 or abs(offset) >= PLANE


def add_bias(st, bias):
    top = jnp.concatenate([st[:BLK, :BLK] + bias[0][0], st[:BLK, BLK:] + bias[0][1]], axis=1)
    low = jnp.concatenate([st[BLK:, :BLK] + bias[1][0], st[BLK:, BLK:] + bias[1][1]], axis=1)
    return jnp.concatenate([top, low], axis=0)


def bias_of(mask, q_group, k_group, valid):
    return [
        [
            jnp.where(valid & (mask[2 * q_group + qb, 2 * k_group + kb] != 0), 0.0, NEG)
            for qb in range(2)
        ]
        for kb in range(2)
    ]


def fetch(parts, pool, sems, wholes=(), only_x=False):
    copies = []
    at = 0
    for n, ref in enumerate(parts):
        size = ref.shape[0]
        for first, count in (((0, 1), (5, 1)) if only_x else ((0, size),)):
            if first < size:
                copies.append(
                    pltpu.make_async_copy(
                        ref.at[pl.ds(first, count)],
                        pool.at[pl.ds(at + first, count)],
                        sems.at[2 * n + (first > 0)],
                    )
                )
        at += size
    for n, (whole, target) in enumerate(wholes):
        copies.append(pltpu.make_async_copy(whole, target, sems.at[2 * PARTS + n]))
    far_count = len(copies) - len(wholes)
    for copy in copies[far_count:] + copies[:far_count]:
        copy.start()
    for copy in copies[far_count:]:
        copy.wait()

    def rest():
        for copy in copies[:far_count]:
            copy.wait()

    return rest


def near(ref, z, unit, which):
    return ref[z, :, jnp.where(unit == 4, 1, 0), which].reshape(TOK, E)


def far(ref, slot, which):
    return ref[slot, :, which].reshape(TOK, E)


def turn_rows(frames, rates, block):
    angles = frames[block].astype(F32) * rates[0:1]
    sine = jnp.sin(angles)
    return jnp.cos(angles), sine * rates[1:2], sine * rates[2:3]


def unturn(x, frames, rates, group):
    halves = []
    for blk in range(2):
        c, s1, s2 = turn_rows(frames, rates, 2 * group + blk)
        halves.append(turn(x[blk * BLK : (blk + 1) * BLK], c, -s1, -s2))
    return jnp.concatenate(halves, axis=0)


def put(ref, at, which, val):
    for b in range(4):
        ref[at, b, which] = val[b * QTR : (b + 1) * QTR]


def read_stats(ref, unit, *at):
    rows = [ref[(*at, pl.ds(4 * unit + n, 1), slice(None))] for n in range(4)]
    return jnp.concatenate(rows[:2], axis=1), jnp.concatenate(rows[2:], axis=1)


def pool_rows(offset, slot, unit, near_ref, pool, which):
    if local(offset):
        return near(near_ref, slot, unit, which)
    return far(pool, slot, which)


def forward_kernel(pos, *refs):
    parts, wholes, others = refs[:PARTS], refs[PARTS : PARTS + 3], refs[PARTS + 3 :]
    att_ref, stats, pool, sems, mask, kv, qg, scores, weights, values = others
    rest = fetch(parts, pool, sems, list(zip(wholes, (mask, kv, qg))))
    zh, p = pos[0], pos[1]

    def body(unit, carry):
        z = jnp.where(unit == 4, zh, unit)
        q = near(qg, z, unit, 0)
        slots = []
        top = jnp.full((1, TOK), NEG, F32)
        for n, offset in enumerate(OFFSETS):
            if offset == FIRST_FAR:
                pl.when(unit == 0)(rest)
            group, other, valid, slot = source(offset, unit, zh, p)
            slots.append(slot)
            k = pool_rows(offset, slot, unit, kv, pool, 0)
            st = add_bias(dot(k, q, 1, 1), bias_of(mask, group, other, valid))
            scores[n] = st
            top = jnp.maximum(top, jnp.max(st, axis=0, keepdims=True))
        top = top * COEF
        total = jnp.zeros((1, TOK), F32)
        for n, offset in enumerate(OFFSETS):
            w = jnp.exp2(scores[n] * COEF - top)
            total = total + jnp.sum(w, axis=0, keepdims=True)
            rows = slice(n * TOK, (n + 1) * TOK)
            weights[rows] = w.astype(BF16)
            values[rows] = pool_rows(offset, slots[n], unit, kv, pool, 1)
        out = dot(values[...], weights[...], 0, 0)
        att = jnp.transpose(out * (1.0 / total)).astype(BF16)
        put(att_ref, unit, 0, att)
        g = near(qg, z, unit, 1).astype(F32)
        delta = jnp.sum(jnp.transpose(g * att.astype(F32)), axis=0, keepdims=True)
        for n, row in enumerate((top + jnp.log2(total), delta)):
            stats[pl.ds(4 * unit + 2 * n, 1), :] = row[:, :BLK]
            stats[pl.ds(4 * unit + 2 * n + 1, 1), :] = row[:, BLK:]
        return carry

    stats[...] = jnp.zeros_like(stats)
    lax.fori_loop(0, UNITS, body, 0)


def query_kernel(pos, frames, rates, *refs):
    parts, wholes, others = refs[:PARTS], refs[PARTS : PARTS + 5], refs[PARTS + 5 :]
    m_ref, x_ref, pool, sems, mask, kv, qg, att, stats, dscores, keys, values, scores, products = others
    rest = fetch(parts, pool, sems, list(zip(wholes, (mask, kv, qg, att, stats))))
    zh, p = pos[0], pos[1]

    def body(unit, carry):
        z = jnp.where(unit == 4, zh, unit)
        q = near(qg, z, unit, 0)
        g = near(qg, z, unit, 1)
        total, delta = read_stats(stats, unit)
        for n, offset in enumerate(OFFSETS):
            if offset == FIRST_FAR:
                pl.when(unit == 0)(rest)
            slot = source(offset, unit, zh, p)[3]
            keys[n * TOK : (n + 1) * TOK] = pool_rows(offset, slot, unit, kv, pool, 0)
            values[n * TOK : (n + 1) * TOK] = pool_rows(offset, slot, unit, kv, pool, 1)
        scores[...] = dot(keys[...], q, 1, 1)
        products[...] = dot(values[...], g, 1, 1)
        for n, offset in enumerate(OFFSETS):
            group, other, valid, _ = source(offset, unit, zh, p)
            rows = slice(n * TOK, (n + 1) * TOK)
            st = add_bias(scores[rows], bias_of(mask, group, other, valid))
            w = jnp.exp2(st * COEF - total)
            dscores[rows] = (w * (products[rows] - delta)).astype(BF16)
        dq = dot(keys[...], dscores[...], 0, 0)
        dq = unturn(jnp.transpose(dq * SCALE), frames, rates, z * PLANE + p).astype(BF16)

        @pl.when(unit < 4)
        def _():
            m_ref[unit, :, 0] = att[unit, :, 0]
            put(m_ref, unit, 1, dq)

        @pl.when(unit == 4)
        def _():
            x_ref[0, :, 0] = att[4, :, 0]
            put(x_ref, 0, 1, dq)

        return carry

    lax.fori_loop(0, UNITS, body, 0)


def key_terms(unit, zh, p, mask, kv, qg, pool, stats_of, rest, big):
    z = jnp.where(unit == 4, zh, unit)
    k = near(kv, z, unit, 0)
    v = near(kv, z, unit, 1)
    weights, dscores, queries, grads = big
    for n, offset in enumerate(OFFSETS):
        if offset == FIRST_FAR:
            rest()
        group, other, valid, slot = source(offset, unit, zh, p)
        total, delta = stats_of(other)
        q = pool_rows(offset, slot, unit, qg, pool, 0)
        g = pool_rows(offset, slot, unit, qg, pool, 1)
        st = add_bias(dot(k, q, 1, 1), bias_of(mask, other, group, valid))
        w = jnp.exp2(st * COEF - total)
        cols = slice(n * TOK, (n + 1) * TOK)
        weights[:, cols] = w.astype(BF16)
        dscores[:, cols] = (w * (dot(v, g, 1, 1) - delta)).astype(BF16)
        queries[cols] = q
        grads[cols] = g
    return dot(dscores[...], queries[...], 1, 0), dot(weights[...], grads[...], 1, 0)


def key_kernel(pos, frames, rates, *refs):
    parts, wholes, others = refs[:PARTS], refs[PARTS : PARTS + 4], refs[PARTS + 4 :]
    o_ref, pool, sems, mask, kv, qg, stats, *big = others
    rest = fetch(parts, pool, sems, list(zip(wholes, (mask, kv, qg, stats))))
    zh, p = pos[0], pos[1]

    def stats_of(other):
        return read_stats(stats, lax.div(other, PLANE), zh * PLANE + lax.rem(other, PLANE))

    def body(unit, carry):
        dk, dv = key_terms(
            unit, zh, p, mask, kv, qg, pool, stats_of, lambda: pl.when(unit == 0)(rest), big
        )
        dk = unturn(dk * SCALE, frames, rates, unit * PLANE + p)
        put(o_ref, unit, 0, dk.astype(BF16))
        put(o_ref, unit, 1, dv.astype(BF16))
        return carry

    lax.fori_loop(0, ZG, body, 0)


def extra_key_kernel(pos, frames, rates, *refs):
    parts, wholes, others = refs[:PARTS], refs[PARTS : PARTS + 5], refs[PARTS + 5 :]
    *pieces, pool, sems, mask, kv, qg, stats, done, c0, c1, c2, c3, sums = others
    big = (c0, c1, c2, c3)
    rest = fetch(parts, pool, sems, list(zip(wholes, (mask, kv, qg, stats, done))), only_x=True)
    zh, p, h = pos[0], pos[1], pos[2]

    def stats_of(other):
        return read_stats(stats, 4, other)

    dk, dv = key_terms(jnp.int32(4), zh, p, mask, kv, qg, pool, stats_of, rest, big)
    put(sums, 0, 0, unturn(dk * SCALE, frames, rates, zh * PLANE + p).astype(BF16))
    put(sums, 0, 1, dv.astype(BF16))
    for n, piece in enumerate(pieces):
        to = lax.rem(h + n, 4)
        for i in range(2):
            piece[i] = done[0, to, i]
            piece[2 + i] = sums[0, to, i]


def cost(pairs, products):
    return pl.CostEstimate(
        flops=pairs * products * 2 * TOK * TOK * E,
        bytes_accessed=8 * 2**20,
        transcendentals=pairs * TOK * TOK,
    )


LIMIT = pltpu.CompilerParams(vmem_limit_bytes=60 * 2**20)


POOL = [
    pltpu.VMEM((SLOTS, 4, 2, QTR, E), BF16),
    pltpu.SemaphoreType.DMA((2 * PARTS + 5,)),
    pltpu.SMEM((2 * GROUPS, 2 * GROUPS), jnp.int32),
    pltpu.VMEM((4, 4, 2, 2, QTR, E), BF16),
    pltpu.VMEM((4, 4, 2, 2, QTR, E), BF16),
]
ALL_SUMS = pltpu.VMEM((len(OFFSETS) * TOK, TOK), F32)
ALL_PAIRS = pltpu.VMEM((len(OFFSETS) * TOK, TOK), BF16)
ALL_ROWS = pltpu.VMEM((len(OFFSETS) * TOK, E), BF16)
ALL_COLUMNS = pltpu.VMEM((TOK, len(OFFSETS) * TOK), BF16)
BIG = [ALL_COLUMNS, ALL_COLUMNS, ALL_ROWS, ALL_ROWS]
EVERY = pltpu.VMEM((GROUPS, SROWS, E), F32)


def side(kernel, out_shape, scratch, pairs, products, scalars, arrays):
    outs = out_shape if isinstance(out_shape, tuple) else (out_shape,)
    specs = [SMEM, SMEM, VMEM][: len(scalars)]
    return pl.pallas_call(
        kernel,
        out_shape=out_shape,
        in_specs=specs + [HBM] * len(arrays),
        out_specs=(VMEM,) * len(outs) if isinstance(out_shape, tuple) else VMEM,
        scratch_shapes=POOL + scratch,
        compiler_params=LIMIT,
        cost_estimate=cost(pairs, products),
        name=kernel.__name__,
    )(*scalars, *arrays)


def blocks(units, tensors):
    return jax.ShapeDtypeStruct((units, 4, tensors, QTR, E), BF16)


def forward_side(pos, mask, kv, qg, parts):
    shapes = (blocks(UNITS, 1), jax.ShapeDtypeStruct((SROWS, E), F32))
    scratch = [pltpu.VMEM((len(OFFSETS), TOK, TOK), F32), ALL_PAIRS, ALL_ROWS]
    return side(forward_kernel, shapes, scratch, 65, 2, (pos,), (*parts, mask, kv, qg))


def query_side(scalars, mask, kv, qg, att, stats, parts):
    scratch = [pltpu.VMEM((UNITS, 4, 1, QTR, E), BF16), pltpu.VMEM((SROWS, E), F32)]
    scratch += [ALL_PAIRS, ALL_ROWS, ALL_ROWS, ALL_SUMS, ALL_SUMS]
    arrays = (*parts, mask, kv, qg, att, stats)
    return side(query_kernel, (blocks(ZG, 2), blocks(1, 2)), scratch, 65, 3, scalars, arrays)


def key_side(scalars, mask, kv, qg, stats, parts):
    return side(
        key_kernel, blocks(ZG, 2), [EVERY] + BIG, 52, 4, scalars, (*parts, mask, kv, qg, stats)
    )


def extra_key_side(scalars, mask, kv, qg, stats, done, parts):
    pieces = (jax.ShapeDtypeStruct((4, QTR, E), BF16),) * 4
    pair = pltpu.VMEM((1, 4, 2, QTR, E), BF16)
    arrays = (*parts, mask, kv, qg, stats, done)
    return side(extra_key_kernel, pieces, [EVERY, pair] + BIG + [pair], 13, 4, scalars, arrays)


def turn_rates():
    rates = np.zeros((8, E), np.float32)
    rates[0, :HALF] = 10000.0 ** (-2.0 * np.arange(HALF, dtype=np.float32) / ROT)
    rates[0, HALF:ROT] = rates[0, :HALF]
    rates[1, HALF:ROT] = 1.0
    rates[2, :HALF] = -1.0
    return rates


def move(value, rule):
    pairs = []
    for y in range(4):
        for x in range(4):
            to = rule(x, y)
            if to is not None:
                pairs.append((4 * y + x, 4 * (to[1] % 4) + to[0] % 4))
    return lax.ppermute(value, "p", pairs)


def start_exchange(own):
    across = move(own, lambda x, y: (x + 2, y))
    up = move(own, lambda x, y: (x, y + 1))
    down = move(own, lambda x, y: (x, y - 1))
    return up, down, across


def end_exchange(own5, up, down, across, turned):
    eight = move(turned, lambda x, y: (x, y - 1) if x < 2 else (x, y + 1))
    aslant = move(across, lambda x, y: (x, y + 1) if x < 2 else (x, y - 1))
    wrap = move(turned, lambda x, y: (3 - x, y) if x in (0, 3) else None)
    left = move(own5, lambda x, y: (x + 1, y) if x < 3 else None)
    right = move(own5, lambda x, y: (x - 1, y) if x > 0 else None)
    return up, down, eight, across, aslant, wrap, left, right


def slots_of(m, x, zh, p):
    first = lax.dynamic_slice_in_dim(x, zh, 1, axis=0)
    wrap = jnp.clip(zh + jnp.where(p < 8, 1, -1), 0, ZG - 1)
    return jnp.concatenate([first, m, lax.dynamic_slice_in_dim(x, wrap, 1, axis=0)], axis=0)


def gather_heads(packed):
    wide = lax.all_to_all(packed, ("zh", "h"), 0, 0, tiled=True)
    return wide.reshape(4, 4, 2, 2, QTR, E)


def shards(queries, key_vectors, value_vectors, grad_output, block_mask, block_frame):
    zh, p, h = lax.axis_index("zh"), lax.axis_index("p"), lax.axis_index("h")
    pos = jnp.stack([zh, p, h]).astype(jnp.int32)
    rates = turn_rates()
    low = lax.rem(p, 4) < 2
    kv = gather_heads(pack(pos, block_frame, rates, key_vectors, value_vectors))
    qg = pack(pos, block_frame, rates, queries, grad_output)
    kv_own = slots_of(kv[:, :, 0], kv[:, :, 1], zh, p)
    up, down, across = start_exchange(kv_own)
    qg, up, down, across = lax.optimization_barrier((qg, up, down, across))
    kv_parts = end_exchange(kv_own[:5], up, down, across, jnp.where(low, down, up))
    qg = gather_heads(qg)
    qg_own = slots_of(qg[:, :, 0], qg[:, :, 1], zh, p)
    qg_own, kv_some = lax.optimization_barrier((qg_own, kv_parts[2:6]))
    kv_parts = kv_parts[:2] + tuple(kv_some) + kv_parts[6:]
    up, down, across = start_exchange(qg_own)
    att, stats = forward_side(pos, block_mask, kv, qg, kv_parts)
    turned = jnp.where(low, down, up)
    own5, turned, across, att, stats = lax.optimization_barrier(
        (qg_own[:5], turned, across, att, stats)
    )
    qg_parts = end_exchange(own5, up, down, across, turned)
    every = lax.all_to_all(
        jnp.broadcast_to(stats[None], (GROUPS, SROWS, E)), ("zh", "p"), 0, 0, tiled=True
    )
    scalars = (pos, block_frame, rates)
    am, ax = query_side(scalars, block_mask, kv, qg, att, stats, kv_parts)
    am, ax, every, qg_parts = lax.optimization_barrier((am, ax, every, qg_parts))
    bm = key_side(scalars, block_mask, kv, qg, every, qg_parts)
    out = lax.all_to_all(am.reshape(16, 2, QTR, E), ("zh", "h"), 0, 0, tiled=True)
    out, bm = lax.optimization_barrier((out, bm))
    pieces = list(extra_key_side(scalars, block_mask, kv, qg, every, ax, qg_parts))
    for n in range(1, 4):
        pieces[n] = lax.ppermute(pieces[n], "h", [(i, (i + n) % 4) for i in range(4)])
    bm = lax.all_to_all(bm.reshape(16, 2, QTR, E), ("zh", "h"), 0, 0, tiled=True)
    return unpack(pos, out, bm, pieces)


def solution(mesh):
    fine = Mesh(mesh.devices.reshape(ZG, PLANE, 4), ("zh", "p", "h"))
    tok = P(("zh", "p", "h"), None, None)
    return jax.shard_map(
        shards,
        mesh=fine,
        in_specs=(tok, tok, tok, tok, P(), P()),
        out_specs=(tok, tok, tok, tok),
        check_vma=False,
    )
```

```python
import functools
import math

import jax
import jax.numpy as jnp
import numpy as np
from jax import lax
from jax.experimental import pallas as pl
from jax.experimental.pallas import tpu as pltpu
from jax.sharding import Mesh, PartitionSpec as P

ROT = 44
HALF = ROT // 2
BLK = 128
E = 128
TOK = 256
QTR = 64
GROUPS = 64
PLANE = 16
ZG = 4
UNITS = 5
SROWS = 24
NEG = -1e30
PARTS = 8
OFFSETS = (0, 16, -16, 32, -32, 4, -4, 8, -8, 1, -1, 2, -2)
FIRST_FAR = 4
SLOTS = 48
SCALE = 1.0 / math.sqrt(E)
LOG2E = 1.4426950408889634
COEF = SCALE * LOG2E
F32 = jnp.float32
BF16 = jnp.bfloat16
HBM = pl.BlockSpec(memory_space=pltpu.HBM)
SMEM = pl.BlockSpec(memory_space=pltpu.SMEM)
VMEM = pl.BlockSpec(memory_space=pltpu.VMEM)

WIDE = jax.ShapeDtypeStruct((16, 2, 2, QTR, E), BF16)


def dot(a, b, ca, cb):
    return lax.dot_general(a, b, (((ca,), (cb,)), ((), ())), preferred_element_type=F32)


def turn(x, c, s1, s2):
    return x * c + pltpu.roll(x, HALF, x.ndim - 1) * s1 + pltpu.roll(x, E - HALF, x.ndim - 1) * s2


def pack_kernel(pos, frames, rates, a_hbm, b_hbm, o_ref, a_ref, b_ref, sems):
    copies = [
        pltpu.make_async_copy(a_hbm, a_ref, sems.at[0]),
        pltpu.make_async_copy(b_hbm, b_ref, sems.at[1]),
    ]
    for copy in copies:
        copy.start()
    block = 2 * (pos[0] * PLANE + pos[1]) + pos[2] // 2
    rows = [r[None] for r in turn_rows(frames, rates, block)]
    copies[0].wait()
    a = turn(a_ref[...].astype(F32), *rows).astype(BF16)
    copies[1].wait()
    for n, val in ((0, a), (1, b_ref[...])):
        o_ref[:, 0, n] = val[:16]
        for i in range(4):
            o_ref[4 * i : 4 * i + 4, 1, n] = val[16:]


def pack(pos, frames, rates, *tensors):
    return pl.pallas_call(
        pack_kernel,
        out_shape=WIDE,
        in_specs=[SMEM, SMEM, VMEM, HBM, HBM],
        out_specs=VMEM,
        scratch_shapes=[
            pltpu.VMEM((20, QTR, E), BF16),
            pltpu.VMEM((20, QTR, E), BF16),
            pltpu.SemaphoreType.DMA((2,)),
        ],
        compiler_params=LIMIT,
        name="pack",
    )(pos, frames, rates, *[jnp.transpose(t, (1, 0, 2)) for t in tensors])


def unpack_kernel(pos, a_ref, b_ref, *refs):
    pieces, outs = refs[:4], refs[4:]
    for i, o in enumerate(outs):
        o[:16] = (a_ref, b_ref)[i // 2][:, i % 2]
        for n, piece in enumerate(pieces):
            o[16 + lax.rem(pos[2] - n + 4, 4)] = piece[i]


def unpack(pos, a, b, pieces):
    shape = jax.ShapeDtypeStruct((20, QTR, E), BF16)
    outs = pl.pallas_call(
        unpack_kernel,
        out_shape=(shape,) * 4,
        in_specs=[SMEM] + [VMEM] * 6,
        out_specs=(VMEM,) * 4,
        compiler_params=LIMIT,
        name="unpack",
    )(pos, a, b, *pieces)
    return tuple(jnp.transpose(o, (1, 0, 2)) for o in outs)


def source(offset, unit, zh, p):
    is_x = unit == 4
    z = jnp.where(is_x, zh, unit)
    group = z * PLANE + p
    other = group - offset
    valid = (other >= 0) & (other < GROUPS)
    if local(offset):
        slot = jnp.clip(z - offset // PLANE, 0, ZG - 1)
    else:
        x = lax.rem(p, 4)
        low = x < 2
        base = {
            4: lambda: 0,
            -4: lambda: 6,
            8: lambda: 12,
            -8: lambda: 12,
            1: lambda: jnp.where(x == 0, 30, 36),
            -1: lambda: jnp.where(x == 3, 30, 42),
            2: lambda: jnp.where(low, 24, 18),
            -2: lambda: jnp.where(low, 18, 24),
        }[offset]()
        at = p - offset
        step = jnp.where(at < 0, -1, jnp.where(at >= PLANE, 1, 0))
        zz = jnp.clip(z + step, 0, ZG - 1)
        slot = base + jnp.where(is_x, 5 * step * step, 1 + zz)
    return group, jnp.clip(other, 0, GROUPS - 1), valid, slot


def local(offset):
    return offset == 0 or abs(offset) >= PLANE


def add_bias(st, bias):
    top = jnp.concatenate([st[:BLK, :BLK] + bias[0][0], st[:BLK, BLK:] + bias[0][1]], axis=1)
    low = jnp.concatenate([st[BLK:, :BLK] + bias[1][0], st[BLK:, BLK:] + bias[1][1]], axis=1)
    return jnp.concatenate([top, low], axis=0)


def bias_of(mask, q_group, k_group, valid):
    return [
        [
            jnp.where(valid & (mask[2 * q_group + qb, 2 * k_group + kb] != 0), 0.0, NEG)
            for qb in range(2)
        ]
        for kb in range(2)
    ]


def fetch(parts, pool, sems, wholes=(), only_x=False):
    copies = []
    for n, ref in enumerate(parts):
        at = 6 * n
        size = ref.shape[0]
        for first, count in (((0, 1), (5, 1)) if only_x else ((0, size),)):
            if first < size:
                copies.append(
                    pltpu.make_async_copy(
                        ref.at[pl.ds(first, count)],
                        pool.at[pl.ds(at + first, count)],
                        sems.at[2 * n + (first > 0)],
                    )
                )
    for n, (whole, target) in enumerate(wholes):
        copies.append(pltpu.make_async_copy(whole, target, sems.at[2 * PARTS + n]))
    far_count = len(copies) - len(wholes)
    for copy in copies[far_count:] + copies[:far_count]:
        copy.start()
    for copy in copies[far_count:]:
        copy.wait()

    def rest():
        for copy in copies[:far_count]:
            copy.wait()

    return rest


def near(ref, z, unit, which):
    return ref[z, :, jnp.where(unit == 4, 1, 0), which].reshape(TOK, E)


def far(ref, slot, which):
    return ref[slot, :, which].reshape(TOK, E)


def turn_rows(frames, rates, block):
    angles = frames[block].astype(F32) * rates[0:1]
    sine = jnp.sin(angles)
    return jnp.cos(angles), sine * rates[1:2], sine * rates[2:3]


def unturn(x, frames, rates, group):
    halves = []
    for blk in range(2):
        c, s1, s2 = turn_rows(frames, rates, 2 * group + blk)
        halves.append(turn(x[blk * BLK : (blk + 1) * BLK], c, -s1, -s2))
    return jnp.concatenate(halves, axis=0)


def put(ref, at, which, val):
    for b in range(4):
        ref[at, b, which] = val[b * QTR : (b + 1) * QTR]


def read_stats(ref, unit, *at):
    rows = [ref[(*at, pl.ds(4 * unit + n, 1), slice(None))] for n in range(4)]
    return jnp.concatenate(rows[:2], axis=1), jnp.concatenate(rows[2:], axis=1)


def pool_rows(offset, slot, unit, near_ref, pool, which):
    if local(offset):
        return near(near_ref, slot, unit, which)
    return far(pool, slot, which)


def forward_kernel(pos, *refs):
    parts, wholes, others = refs[:PARTS], refs[PARTS : PARTS + 3], refs[PARTS + 3 :]
    att_ref, stats, pool, sems, mask, kv, qg, scores, weights, values = others
    rest = fetch(parts, pool, sems, list(zip(wholes, (mask, kv, qg))))
    zh, p = pos[0], pos[1]

    def body(unit, carry):
        z = jnp.where(unit == 4, zh, unit)
        q = near(qg, z, unit, 0)
        slots = []
        top = jnp.full((1, TOK), NEG, F32)
        for n, offset in enumerate(OFFSETS):
            if offset == FIRST_FAR:
                pl.when(unit == 0)(rest)
            group, other, valid, slot = source(offset, unit, zh, p)
            slots.append(slot)
            k = pool_rows(offset, slot, unit, kv, pool, 0)
            st = add_bias(dot(k, q, 1, 1), bias_of(mask, group, other, valid))
            scores[n] = st
            top = jnp.maximum(top, jnp.max(st, axis=0, keepdims=True))
        top = top * COEF
        total = jnp.zeros((1, TOK), F32)
        for n, offset in enumerate(OFFSETS):
            w = jnp.exp2(scores[n] * COEF - top)
            total = total + jnp.sum(w, axis=0, keepdims=True)
            rows = slice(n * TOK, (n + 1) * TOK)
            weights[rows] = w.astype(BF16)
            values[rows] = pool_rows(offset, slots[n], unit, kv, pool, 1)
        out = dot(values[...], weights[...], 0, 0)
        att = jnp.transpose(out * (1.0 / total)).astype(BF16)
        put(att_ref, unit, 0, att)
        g = near(qg, z, unit, 1).astype(F32)
        delta = jnp.sum(jnp.transpose(g * att.astype(F32)), axis=0, keepdims=True)
        for n, row in enumerate((top + jnp.log2(total), delta)):
            stats[pl.ds(4 * unit + 2 * n, 1), :] = row[:, :BLK]
            stats[pl.ds(4 * unit + 2 * n + 1, 1), :] = row[:, BLK:]
        return carry

    stats[...] = jnp.zeros_like(stats)
    lax.fori_loop(0, UNITS, body, 0)


def query_kernel(pos, frames, rates, *refs):
    parts, wholes, others = refs[:PARTS], refs[PARTS : PARTS + 5], refs[PARTS + 5 :]
    m_ref, x_ref, pool, sems, mask, kv, qg, att, stats, dscores, keys, values, scores, products = others
    rest = fetch(parts, pool, sems, list(zip(wholes, (mask, kv, qg, att, stats))))
    zh, p = pos[0], pos[1]

    def body(unit, carry):
        z = jnp.where(unit == 4, zh, unit)
        q = near(qg, z, unit, 0)
        g = near(qg, z, unit, 1)
        total, delta = read_stats(stats, unit)
        for n, offset in enumerate(OFFSETS):
            if offset == FIRST_FAR:
                pl.when(unit == 0)(rest)
            slot = source(offset, unit, zh, p)[3]
            keys[n * TOK : (n + 1) * TOK] = pool_rows(offset, slot, unit, kv, pool, 0)
            values[n * TOK : (n + 1) * TOK] = pool_rows(offset, slot, unit, kv, pool, 1)
        scores[...] = dot(keys[...], q, 1, 1)
        products[...] = dot(values[...], g, 1, 1)
        for n, offset in enumerate(OFFSETS):
            group, other, valid, _ = source(offset, unit, zh, p)
            rows = slice(n * TOK, (n + 1) * TOK)
            st = add_bias(scores[rows], bias_of(mask, group, other, valid))
            w = jnp.exp2(st * COEF - total)
            dscores[rows] = (w * (products[rows] - delta)).astype(BF16)
        dq = dot(keys[...], dscores[...], 0, 0)
        dq = unturn(jnp.transpose(dq * SCALE), frames, rates, z * PLANE + p).astype(BF16)

        @pl.when(unit < 4)
        def _():
            m_ref[unit, :, 0] = att[unit, :, 0]
            put(m_ref, unit, 1, dq)

        @pl.when(unit == 4)
        def _():
            x_ref[0, :, 0] = att[4, :, 0]
            put(x_ref, 0, 1, dq)

        return carry

    lax.fori_loop(0, UNITS, body, 0)


def key_terms(unit, zh, p, mask, kv, qg, pool, stats_of, rest, big):
    z = jnp.where(unit == 4, zh, unit)
    k = near(kv, z, unit, 0)
    v = near(kv, z, unit, 1)
    weights, dscores, queries, grads = big
    for n, offset in enumerate(OFFSETS):
        if offset == FIRST_FAR:
            rest()
        group, other, valid, slot = source(offset, unit, zh, p)
        total, delta = stats_of(other)
        q = pool_rows(offset, slot, unit, qg, pool, 0)
        g = pool_rows(offset, slot, unit, qg, pool, 1)
        st = add_bias(dot(k, q, 1, 1), bias_of(mask, other, group, valid))
        w = jnp.exp2(st * COEF - total)
        cols = slice(n * TOK, (n + 1) * TOK)
        weights[:, cols] = w.astype(BF16)
        dscores[:, cols] = (w * (dot(v, g, 1, 1) - delta)).astype(BF16)
        queries[cols] = q
        grads[cols] = g
    return dot(dscores[...], queries[...], 1, 0), dot(weights[...], grads[...], 1, 0)


def key_kernel(pos, frames, rates, *refs):
    parts, wholes, others = refs[:PARTS], refs[PARTS : PARTS + 4], refs[PARTS + 4 :]
    o_ref, pool, sems, mask, kv, qg, stats, *big = others
    rest = fetch(parts, pool, sems, list(zip(wholes, (mask, kv, qg, stats))))
    zh, p = pos[0], pos[1]

    def stats_of(other):
        return read_stats(stats, lax.div(other, PLANE), zh * PLANE + lax.rem(other, PLANE))

    def body(unit, carry):
        dk, dv = key_terms(
            unit, zh, p, mask, kv, qg, pool, stats_of, lambda: pl.when(unit == 0)(rest), big
        )
        dk = unturn(dk * SCALE, frames, rates, unit * PLANE + p)
        put(o_ref, unit, 0, dk.astype(BF16))
        put(o_ref, unit, 1, dv.astype(BF16))
        return carry

    lax.fori_loop(0, ZG, body, 0)


def extra_key_kernel(pos, frames, rates, *refs):
    parts, wholes, others = refs[:PARTS], refs[PARTS : PARTS + 5], refs[PARTS + 5 :]
    *pieces, pool, sems, mask, kv, qg, stats, done, c0, c1, c2, c3, sums = others
    big = (c0, c1, c2, c3)
    rest = fetch(parts, pool, sems, list(zip(wholes, (mask, kv, qg, stats, done))), only_x=True)
    zh, p, h = pos[0], pos[1], pos[2]

    def stats_of(other):
        return read_stats(stats, 4, other)

    dk, dv = key_terms(jnp.int32(4), zh, p, mask, kv, qg, pool, stats_of, rest, big)
    put(sums, 0, 0, unturn(dk * SCALE, frames, rates, zh * PLANE + p).astype(BF16))
    put(sums, 0, 1, dv.astype(BF16))
    for n, piece in enumerate(pieces):
        to = lax.rem(h + n, 4)
        for i in range(2):
            piece[i] = done[0, to, i]
            piece[2 + i] = sums[0, to, i]


def cost(pairs, products):
    return pl.CostEstimate(
        flops=pairs * products * 2 * TOK * TOK * E,
        bytes_accessed=8 * 2**20,
        transcendentals=pairs * TOK * TOK,
    )


LIMIT = pltpu.CompilerParams(vmem_limit_bytes=60 * 2**20)


POOL = [
    pltpu.VMEM((SLOTS, 4, 2, QTR, E), BF16),
    pltpu.SemaphoreType.DMA((2 * PARTS + 5,)),
    pltpu.SMEM((2 * GROUPS, 2 * GROUPS), jnp.int32),
    pltpu.VMEM((4, 4, 2, 2, QTR, E), BF16),
    pltpu.VMEM((4, 4, 2, 2, QTR, E), BF16),
]
ALL_SUMS = pltpu.VMEM((len(OFFSETS) * TOK, TOK), F32)
ALL_PAIRS = pltpu.VMEM((len(OFFSETS) * TOK, TOK), BF16)
ALL_ROWS = pltpu.VMEM((len(OFFSETS) * TOK, E), BF16)
ALL_COLUMNS = pltpu.VMEM((TOK, len(OFFSETS) * TOK), BF16)
BIG = [ALL_COLUMNS, ALL_COLUMNS, ALL_ROWS, ALL_ROWS]
EVERY = pltpu.VMEM((GROUPS, SROWS, E), F32)


def side(kernel, out_shape, scratch, pairs, products, scalars, arrays):
    outs = out_shape if isinstance(out_shape, tuple) else (out_shape,)
    specs = [SMEM, SMEM, VMEM][: len(scalars)]
    return pl.pallas_call(
        kernel,
        out_shape=out_shape,
        in_specs=specs + [HBM] * len(arrays),
        out_specs=(VMEM,) * len(outs) if isinstance(out_shape, tuple) else VMEM,
        scratch_shapes=POOL + scratch,
        compiler_params=LIMIT,
        cost_estimate=cost(pairs, products),
        name=kernel.__name__,
    )(*scalars, *arrays)


def blocks(units, tensors):
    return jax.ShapeDtypeStruct((units, 4, tensors, QTR, E), BF16)


def forward_side(pos, mask, kv, qg, parts):
    shapes = (blocks(UNITS, 1), jax.ShapeDtypeStruct((SROWS, E), F32))
    scratch = [pltpu.VMEM((len(OFFSETS), TOK, TOK), F32), ALL_PAIRS, ALL_ROWS]
    return side(forward_kernel, shapes, scratch, 65, 2, (pos,), (*parts, mask, kv, qg))


def query_side(scalars, mask, kv, qg, att, stats, parts):
    scratch = [pltpu.VMEM((UNITS, 4, 1, QTR, E), BF16), pltpu.VMEM((SROWS, E), F32)]
    scratch += [ALL_PAIRS, ALL_ROWS, ALL_ROWS, ALL_SUMS, ALL_SUMS]
    arrays = (*parts, mask, kv, qg, att, stats)
    return side(query_kernel, (blocks(ZG, 2), blocks(1, 2)), scratch, 65, 3, scalars, arrays)


def key_side(scalars, mask, kv, qg, stats, parts):
    return side(
        key_kernel, blocks(ZG, 2), [EVERY] + BIG, 52, 4, scalars, (*parts, mask, kv, qg, stats)
    )


def extra_key_side(scalars, mask, kv, qg, stats, done, parts):
    pieces = (jax.ShapeDtypeStruct((4, QTR, E), BF16),) * 4
    pair = pltpu.VMEM((1, 4, 2, QTR, E), BF16)
    arrays = (*parts, mask, kv, qg, stats, done)
    return side(extra_key_kernel, pieces, [EVERY, pair] + BIG + [pair], 13, 4, scalars, arrays)


def turn_rates():
    rates = np.zeros((8, E), np.float32)
    rates[0, :HALF] = 10000.0 ** (-2.0 * np.arange(HALF, dtype=np.float32) / ROT)
    rates[0, HALF:ROT] = rates[0, :HALF]
    rates[1, HALF:ROT] = 1.0
    rates[2, :HALF] = -1.0
    return rates


def move(value, rule):
    pairs = []
    for y in range(4):
        for x in range(4):
            to = rule(x, y)
            if to is not None:
                pairs.append((4 * y + x, 4 * (to[1] % 4) + to[0] % 4))
    return lax.ppermute(value, "p", pairs)


def start_exchange(own):
    up = move(own, lambda x, y: (x, y + 1))
    down = move(own, lambda x, y: (x, y - 1))
    across = move(own, lambda x, y: (x + 2, y))
    return up, down, across


def end_exchange(own, up, down, across, turned):
    eight = move(turned, lambda x, y: (x, y - 1) if x < 2 else (x, y + 1))
    aslant = move(across, lambda x, y: (x, y + 1) if x < 2 else (x, y - 1))
    wrap = move(turned, lambda x, y: (3 - x, y) if x in (0, 3) else None)
    left = move(own, lambda x, y: (x + 1, y) if x < 3 else None)
    right = move(own, lambda x, y: (x - 1, y) if x > 0 else None)
    return up, down, eight, across, aslant, wrap, left, right


def slots_of(m, x, zh, p):
    first = lax.dynamic_slice_in_dim(x, zh, 1, axis=0)
    wrap = jnp.clip(zh + jnp.where(p < 8, 1, -1), 0, ZG - 1)
    return jnp.concatenate([first, m, lax.dynamic_slice_in_dim(x, wrap, 1, axis=0)], axis=0)


def gather_heads(packed):
    wide = lax.all_to_all(packed, ("zh", "h"), 0, 0, tiled=True)
    return wide.reshape(4, 4, 2, 2, QTR, E)


def shards(queries, key_vectors, value_vectors, grad_output, block_mask, block_frame):
    zh, p, h = lax.axis_index("zh"), lax.axis_index("p"), lax.axis_index("h")
    pos = jnp.stack([zh, p, h]).astype(jnp.int32)
    rates = turn_rates()
    low = lax.rem(p, 4) < 2
    kv = gather_heads(pack(pos, block_frame, rates, key_vectors, value_vectors))
    qg = pack(pos, block_frame, rates, queries, grad_output)
    kv_own = slots_of(kv[:, :, 0], kv[:, :, 1], zh, p)
    up, down, across = start_exchange(kv_own)
    own5 = kv_own[:5]
    across, down, up, own5, qg = lax.optimization_barrier((across, down, up, own5, qg))
    kv_parts = end_exchange(own5, up, down, across, jnp.where(low, down, up))
    qg = gather_heads(qg)
    qg_own = slots_of(qg[:, :, 0], qg[:, :, 1], zh, p)
    qg_own, kv_some = lax.optimization_barrier((qg_own, kv_parts[2:6]))
    kv_parts = kv_parts[:2] + tuple(kv_some) + kv_parts[6:]
    up, down, across = start_exchange(qg_own)
    att, stats = forward_side(pos, block_mask, kv, qg, kv_parts)
    turned = jnp.where(low, down, up)
    own, turned, across, att, stats = lax.optimization_barrier(
        (qg_own, turned, across, att, stats)
    )
    qg_parts = end_exchange(own, up, down, across, turned)
    every = lax.all_to_all(
        jnp.broadcast_to(stats[None], (GROUPS, SROWS, E)), ("zh", "p"), 0, 0, tiled=True
    )
    scalars = (pos, block_frame, rates)
    am, ax = query_side(scalars, block_mask, kv, qg, att, stats, kv_parts)
    am, every = lax.optimization_barrier((am, every))
    bm = key_side(scalars, block_mask, kv, qg, every, qg_parts)
    out = lax.all_to_all(am.reshape(16, 2, QTR, E), ("zh", "h"), 0, 0, tiled=True)
    out, bm = lax.optimization_barrier((out, bm))
    pieces = list(extra_key_side(scalars, block_mask, kv, qg, every, ax, qg_parts))
    for n in range(1, 4):
        pieces[n] = lax.ppermute(pieces[n], "h", [(i, (i + n) % 4) for i in range(4)])
    bm = lax.all_to_all(bm.reshape(16, 2, QTR, E), ("zh", "h"), 0, 0, tiled=True)
    return unpack(pos, out, bm, pieces)


def solution(mesh):
    fine = Mesh(mesh.devices.reshape(ZG, PLANE, 4), ("zh", "p", "h"))
    tok = P(("zh", "p", "h"), None, None)
    return jax.shard_map(
        shards,
        mesh=fine,
        in_specs=(tok, tok, tok, tok, P(), P()),
        out_specs=(tok, tok, tok, tok),
        check_vma=False,
    )
```

```python
import functools
import math

import jax
import jax.numpy as jnp
import numpy as np
from jax import lax
from jax.experimental import pallas as pl
from jax.experimental.pallas import tpu as pltpu
from jax.sharding import Mesh, PartitionSpec as P

ROT = 44
HALF = ROT // 2
BLK = 128
E = 128
TOK = 256
QTR = 64
GROUPS = 64
PLANE = 16
ZG = 4
UNITS = 5
SROWS = 24
NEG = -1e30
PARTS = 8
OFFSETS = (0, 16, -16, 32, -32, 4, -4, 8, -8, 1, -1, 2, -2)
FIRST_FAR = 4
SLOTS = 48
SCALE = 1.0 / math.sqrt(E)
LOG2E = 1.4426950408889634
COEF = SCALE * LOG2E
F32 = jnp.float32
BF16 = jnp.bfloat16
HBM = pl.BlockSpec(memory_space=pltpu.HBM)
SMEM = pl.BlockSpec(memory_space=pltpu.SMEM)
VMEM = pl.BlockSpec(memory_space=pltpu.VMEM)

WIDE = jax.ShapeDtypeStruct((16, 2, 2, QTR, E), BF16)


def dot(a, b, ca, cb):
    return lax.dot_general(a, b, (((ca,), (cb,)), ((), ())), preferred_element_type=F32)


def turn(x, c, s1, s2):
    return x * c + pltpu.roll(x, HALF, x.ndim - 1) * s1 + pltpu.roll(x, E - HALF, x.ndim - 1) * s2


def pack_kernel(pos, frames, rates, a_hbm, b_hbm, o_ref, a_ref, b_ref, sems):
    copies = [
        pltpu.make_async_copy(a_hbm, a_ref, sems.at[0]),
        pltpu.make_async_copy(b_hbm, b_ref, sems.at[1]),
    ]
    for copy in copies:
        copy.start()
    block = 2 * (pos[0] * PLANE + pos[1]) + pos[2] // 2
    rows = [r[None] for r in turn_rows(frames, rates, block)]
    copies[0].wait()
    a = turn(a_ref[...].astype(F32), *rows).astype(BF16)
    copies[1].wait()
    for n, val in ((0, a), (1, b_ref[...])):
        o_ref[:, 0, n] = val[:16]
        for i in range(4):
            o_ref[4 * i : 4 * i + 4, 1, n] = val[16:]


def pack(pos, frames, rates, *tensors):
    return pl.pallas_call(
        pack_kernel,
        out_shape=WIDE,
        in_specs=[SMEM, SMEM, VMEM, HBM, HBM],
        out_specs=VMEM,
        scratch_shapes=[
            pltpu.VMEM((20, QTR, E), BF16),
            pltpu.VMEM((20, QTR, E), BF16),
            pltpu.SemaphoreType.DMA((2,)),
        ],
        compiler_params=LIMIT,
        name="pack",
    )(pos, frames, rates, *[jnp.transpose(t, (1, 0, 2)) for t in tensors])


def unpack_kernel(pos, a_hbm, b_hbm, *refs):
    pieces, outs, sems = refs[:4], refs[4:8], refs[8]
    copies = []
    for i, o in enumerate(outs):
        main = (a_hbm, b_hbm)[i // 2]
        copies.append(
            pltpu.make_async_copy(main.at[:, i % 2], o.at[pl.ds(0, 16)], sems.at[5 * i])
        )
        for n, piece in enumerate(pieces):
            to = 16 + lax.rem(pos[2] - n + 4, 4)
            copies.append(pltpu.make_async_copy(piece.at[i], o.at[to], sems.at[5 * i + n + 1]))
    for copy in copies:
        copy.start()
    for copy in copies:
        copy.wait()


def unpack(pos, a, b, pieces):
    shape = jax.ShapeDtypeStruct((20, QTR, E), BF16)
    outs = pl.pallas_call(
        unpack_kernel,
        out_shape=(shape,) * 4,
        in_specs=[SMEM] + [pl.BlockSpec(memory_space=pl.ANY)] * 6,
        out_specs=(HBM,) * 4,
        scratch_shapes=[pltpu.SemaphoreType.DMA((20,))],
        compiler_params=pltpu.CompilerParams(vmem_limit_bytes=2**20),
        name="unpack",
    )(pos, a, b, *pieces)
    return tuple(jnp.transpose(o, (1, 0, 2)) for o in outs)


def source(offset, unit, zh, p):
    is_x = unit == 4
    z = jnp.where(is_x, zh, unit)
    group = z * PLANE + p
    other = group - offset
    valid = (other >= 0) & (other < GROUPS)
    if local(offset):
        slot = jnp.clip(z - offset // PLANE, 0, ZG - 1)
    else:
        x = lax.rem(p, 4)
        low = x < 2
        base = {
            4: lambda: 0,
            -4: lambda: 6,
            8: lambda: 12,
            -8: lambda: 12,
            1: lambda: jnp.where(x == 0, 30, 36),
            -1: lambda: jnp.where(x == 3, 30, 42),
            2: lambda: jnp.where(low, 24, 18),
            -2: lambda: jnp.where(low, 18, 24),
        }[offset]()
        at = p - offset
        step = jnp.where(at < 0, -1, jnp.where(at >= PLANE, 1, 0))
        zz = jnp.clip(z + step, 0, ZG - 1)
        slot = base + jnp.where(is_x, 5 * step * step, 1 + zz)
    return group, jnp.clip(other, 0, GROUPS - 1), valid, slot


def local(offset):
    return offset == 0 or abs(offset) >= PLANE


def add_bias(st, bias):
    top = jnp.concatenate([st[:BLK, :BLK] + bias[0][0], st[:BLK, BLK:] + bias[0][1]], axis=1)
    low = jnp.concatenate([st[BLK:, :BLK] + bias[1][0], st[BLK:, BLK:] + bias[1][1]], axis=1)
    return jnp.concatenate([top, low], axis=0)


def bias_of(mask, q_group, k_group, valid):
    return [
        [
            jnp.where(valid & (mask[2 * q_group + qb, 2 * k_group + kb] != 0), 0.0, NEG)
            for qb in range(2)
        ]
        for kb in range(2)
    ]


def fetch(parts, pool, sems, wholes=(), only_x=False):
    copies = []
    for n, ref in enumerate(parts):
        at = 6 * n
        size = ref.shape[0]
        for first, count in (((0, 1), (5, 1)) if only_x else ((0, size),)):
            if first < size:
                copies.append(
                    pltpu.make_async_copy(
                        ref.at[pl.ds(first, count)],
                        pool.at[pl.ds(at + first, count)],
                        sems.at[2 * n + (first > 0)],
                    )
                )
    for n, (whole, target) in enumerate(wholes):
        copies.append(pltpu.make_async_copy(whole, target, sems.at[2 * PARTS + n]))
    far_count = len(copies) - len(wholes)
    for copy in copies[far_count:] + copies[:far_count]:
        copy.start()
    for copy in copies[far_count:]:
        copy.wait()

    def rest():
        for copy in copies[:far_count]:
            copy.wait()

    return rest


def near(ref, z, unit, which):
    return ref[z, :, jnp.where(unit == 4, 1, 0), which].reshape(TOK, E)


def far(ref, slot, which):
    return ref[slot, :, which].reshape(TOK, E)


def turn_rows(frames, rates, block):
    angles = frames[block].astype(F32) * rates[0:1]
    sine = jnp.sin(angles)
    return jnp.cos(angles), sine * rates[1:2], sine * rates[2:3]


def unturn(x, frames, rates, group):
    halves = []
    for blk in range(2):
        c, s1, s2 = turn_rows(frames, rates, 2 * group + blk)
        halves.append(turn(x[blk * BLK : (blk + 1) * BLK], c, -s1, -s2))
    return jnp.concatenate(halves, axis=0)


def put(ref, at, which, val):
    for b in range(4):
        ref[at, b, which] = val[b * QTR : (b + 1) * QTR]


def read_stats(ref, unit, *at):
    rows = [ref[(*at, pl.ds(4 * unit + n, 1), slice(None))] for n in range(4)]
    return jnp.concatenate(rows[:2], axis=1), jnp.concatenate(rows[2:], axis=1)


def pool_rows(offset, slot, unit, near_ref, pool, which):
    if local(offset):
        return near(near_ref, slot, unit, which)
    return far(pool, slot, which)


def forward_kernel(pos, *refs):
    parts, wholes, others = refs[:PARTS], refs[PARTS : PARTS + 3], refs[PARTS + 3 :]
    att_ref, stats, pool, sems, mask, kv, qg, scores, weights, values = others
    rest = fetch(parts, pool, sems, list(zip(wholes, (mask, kv, qg))))
    zh, p = pos[0], pos[1]

    def body(unit, carry):
        z = jnp.where(unit == 4, zh, unit)
        q = near(qg, z, unit, 0)
        slots = []
        top = jnp.full((1, TOK), NEG, F32)
        for n, offset in enumerate(OFFSETS):
            if offset == FIRST_FAR:
                pl.when(unit == 0)(rest)
            group, other, valid, slot = source(offset, unit, zh, p)
            slots.append(slot)
            k = pool_rows(offset, slot, unit, kv, pool, 0)
            st = add_bias(dot(k, q, 1, 1), bias_of(mask, group, other, valid))
            scores[n] = st
            top = jnp.maximum(top, jnp.max(st, axis=0, keepdims=True))
        top = top * COEF
        total = jnp.zeros((1, TOK), F32)
        for n, offset in enumerate(OFFSETS):
            w = jnp.exp2(scores[n] * COEF - top)
            total = total + jnp.sum(w, axis=0, keepdims=True)
            rows = slice(n * TOK, (n + 1) * TOK)
            weights[rows] = w.astype(BF16)
            values[rows] = pool_rows(offset, slots[n], unit, kv, pool, 1)
        out = dot(values[...], weights[...], 0, 0)
        att = jnp.transpose(out * (1.0 / total)).astype(BF16)
        put(att_ref, unit, 0, att)
        g = near(qg, z, unit, 1).astype(F32)
        delta = jnp.sum(jnp.transpose(g * att.astype(F32)), axis=0, keepdims=True)
        for n, row in enumerate((top + jnp.log2(total), delta)):
            stats[pl.ds(4 * unit + 2 * n, 1), :] = row[:, :BLK]
            stats[pl.ds(4 * unit + 2 * n + 1, 1), :] = row[:, BLK:]
        return carry

    stats[...] = jnp.zeros_like(stats)
    lax.fori_loop(0, UNITS, body, 0)


def query_kernel(pos, frames, rates, *refs):
    parts, wholes, others = refs[:PARTS], refs[PARTS : PARTS + 5], refs[PARTS + 5 :]
    m_ref, x_ref, pool, sems, mask, kv, qg, att, stats, dscores, keys, values, scores, products = others
    rest = fetch(parts, pool, sems, list(zip(wholes, (mask, kv, qg, att, stats))))
    zh, p = pos[0], pos[1]

    def body(unit, carry):
        z = jnp.where(unit == 4, zh, unit)
        q = near(qg, z, unit, 0)
        g = near(qg, z, unit, 1)
        total, delta = read_stats(stats, unit)
        for n, offset in enumerate(OFFSETS):
            if offset == FIRST_FAR:
                pl.when(unit == 0)(rest)
            slot = source(offset, unit, zh, p)[3]
            keys[n * TOK : (n + 1) * TOK] = pool_rows(offset, slot, unit, kv, pool, 0)
            values[n * TOK : (n + 1) * TOK] = pool_rows(offset, slot, unit, kv, pool, 1)
        scores[...] = dot(keys[...], q, 1, 1)
        products[...] = dot(values[...], g, 1, 1)
        for n, offset in enumerate(OFFSETS):
            group, other, valid, _ = source(offset, unit, zh, p)
            rows = slice(n * TOK, (n + 1) * TOK)
            st = add_bias(scores[rows], bias_of(mask, group, other, valid))
            w = jnp.exp2(st * COEF - total)
            dscores[rows] = (w * (products[rows] - delta)).astype(BF16)
        dq = dot(keys[...], dscores[...], 0, 0)
        dq = unturn(jnp.transpose(dq * SCALE), frames, rates, z * PLANE + p).astype(BF16)

        @pl.when(unit < 4)
        def _():
            m_ref[unit, :, 0] = att[unit, :, 0]
            put(m_ref, unit, 1, dq)

        @pl.when(unit == 4)
        def _():
            x_ref[0, :, 0] = att[4, :, 0]
            put(x_ref, 0, 1, dq)

        return carry

    lax.fori_loop(0, UNITS, body, 0)


def key_terms(unit, zh, p, mask, kv, qg, pool, stats_of, rest, big):
    z = jnp.where(unit == 4, zh, unit)
    k = near(kv, z, unit, 0)
    v = near(kv, z, unit, 1)
    weights, dscores, queries, grads = big
    for n, offset in enumerate(OFFSETS):
        if offset == FIRST_FAR:
            rest()
        group, other, valid, slot = source(offset, unit, zh, p)
        total, delta = stats_of(other)
        q = pool_rows(offset, slot, unit, qg, pool, 0)
        g = pool_rows(offset, slot, unit, qg, pool, 1)
        st = add_bias(dot(k, q, 1, 1), bias_of(mask, other, group, valid))
        w = jnp.exp2(st * COEF - total)
        cols = slice(n * TOK, (n + 1) * TOK)
        weights[:, cols] = w.astype(BF16)
        dscores[:, cols] = (w * (dot(v, g, 1, 1) - delta)).astype(BF16)
        queries[cols] = q
        grads[cols] = g
    return dot(dscores[...], queries[...], 1, 0), dot(weights[...], grads[...], 1, 0)


def key_kernel(pos, frames, rates, *refs):
    parts, wholes, others = refs[:PARTS], refs[PARTS : PARTS + 4], refs[PARTS + 4 :]
    o_ref, pool, sems, mask, kv, qg, stats, *big = others
    rest = fetch(parts, pool, sems, list(zip(wholes, (mask, kv, qg, stats))))
    zh, p = pos[0], pos[1]

    def stats_of(other):
        return read_stats(stats, lax.div(other, PLANE), zh * PLANE + lax.rem(other, PLANE))

    def body(unit, carry):
        dk, dv = key_terms(
            unit, zh, p, mask, kv, qg, pool, stats_of, lambda: pl.when(unit == 0)(rest), big
        )
        dk = unturn(dk * SCALE, frames, rates, unit * PLANE + p)
        put(o_ref, unit, 0, dk.astype(BF16))
        put(o_ref, unit, 1, dv.astype(BF16))
        return carry

    lax.fori_loop(0, ZG, body, 0)


def extra_key_kernel(pos, frames, rates, *refs):
    parts, wholes, others = refs[:PARTS], refs[PARTS : PARTS + 5], refs[PARTS + 5 :]
    *pieces, pool, sems, mask, kv, qg, stats, done, c0, c1, c2, c3, sums = others
    big = (c0, c1, c2, c3)
    rest = fetch(parts, pool, sems, list(zip(wholes, (mask, kv, qg, stats, done))), only_x=True)
    zh, p, h = pos[0], pos[1], pos[2]

    def stats_of(other):
        return read_stats(stats, 4, other)

    dk, dv = key_terms(jnp.int32(4), zh, p, mask, kv, qg, pool, stats_of, rest, big)
    put(sums, 0, 0, unturn(dk * SCALE, frames, rates, zh * PLANE + p).astype(BF16))
    put(sums, 0, 1, dv.astype(BF16))
    for n, piece in enumerate(pieces):
        to = lax.rem(h + n, 4)
        for i in range(2):
            piece[i] = done[0, to, i]
            piece[2 + i] = sums[0, to, i]


def cost(pairs, products):
    return pl.CostEstimate(
        flops=pairs * products * 2 * TOK * TOK * E,
        bytes_accessed=8 * 2**20,
        transcendentals=pairs * TOK * TOK,
    )


LIMIT = pltpu.CompilerParams(vmem_limit_bytes=60 * 2**20)


POOL = [
    pltpu.VMEM((SLOTS, 4, 2, QTR, E), BF16),
    pltpu.SemaphoreType.DMA((2 * PARTS + 5,)),
    pltpu.SMEM((2 * GROUPS, 2 * GROUPS), jnp.int32),
    pltpu.VMEM((4, 4, 2, 2, QTR, E), BF16),
    pltpu.VMEM((4, 4, 2, 2, QTR, E), BF16),
]
ALL_SUMS = pltpu.VMEM((len(OFFSETS) * TOK, TOK), F32)
ALL_PAIRS = pltpu.VMEM((len(OFFSETS) * TOK, TOK), BF16)
ALL_ROWS = pltpu.VMEM((len(OFFSETS) * TOK, E), BF16)
ALL_COLUMNS = pltpu.VMEM((TOK, len(OFFSETS) * TOK), BF16)
BIG = [ALL_COLUMNS, ALL_COLUMNS, ALL_ROWS, ALL_ROWS]
EVERY = pltpu.VMEM((GROUPS, SROWS, E), F32)


def side(kernel, out_shape, scratch, pairs, products, scalars, arrays):
    outs = out_shape if isinstance(out_shape, tuple) else (out_shape,)
    specs = [SMEM, SMEM, VMEM][: len(scalars)]
    return pl.pallas_call(
        kernel,
        out_shape=out_shape,
        in_specs=specs + [HBM] * len(arrays),
        out_specs=(VMEM,) * len(outs) if isinstance(out_shape, tuple) else VMEM,
        scratch_shapes=POOL + scratch,
        compiler_params=LIMIT,
        cost_estimate=cost(pairs, products),
        name=kernel.__name__,
    )(*scalars, *arrays)


def blocks(units, tensors):
    return jax.ShapeDtypeStruct((units, 4, tensors, QTR, E), BF16)


def forward_side(pos, mask, kv, qg, parts):
    shapes = (blocks(UNITS, 1), jax.ShapeDtypeStruct((SROWS, E), F32))
    scratch = [pltpu.VMEM((len(OFFSETS), TOK, TOK), F32), ALL_PAIRS, ALL_ROWS]
    return side(forward_kernel, shapes, scratch, 65, 2, (pos,), (*parts, mask, kv, qg))


def query_side(scalars, mask, kv, qg, att, stats, parts):
    scratch = [pltpu.VMEM((UNITS, 4, 1, QTR, E), BF16), pltpu.VMEM((SROWS, E), F32)]
    scratch += [ALL_PAIRS, ALL_ROWS, ALL_ROWS, ALL_SUMS, ALL_SUMS]
    arrays = (*parts, mask, kv, qg, att, stats)
    return side(query_kernel, (blocks(ZG, 2), blocks(1, 2)), scratch, 65, 3, scalars, arrays)


def key_side(scalars, mask, kv, qg, stats, parts):
    return side(
        key_kernel, blocks(ZG, 2), [EVERY] + BIG, 52, 4, scalars, (*parts, mask, kv, qg, stats)
    )


def extra_key_side(scalars, mask, kv, qg, stats, done, parts):
    pieces = (jax.ShapeDtypeStruct((4, QTR, E), BF16),) * 4
    pair = pltpu.VMEM((1, 4, 2, QTR, E), BF16)
    arrays = (*parts, mask, kv, qg, stats, done)
    return side(extra_key_kernel, pieces, [EVERY, pair] + BIG + [pair], 13, 4, scalars, arrays)


def turn_rates():
    rates = np.zeros((8, E), np.float32)
    rates[0, :HALF] = 10000.0 ** (-2.0 * np.arange(HALF, dtype=np.float32) / ROT)
    rates[0, HALF:ROT] = rates[0, :HALF]
    rates[1, HALF:ROT] = 1.0
    rates[2, :HALF] = -1.0
    return rates


def move(value, rule):
    pairs = []
    for y in range(4):
        for x in range(4):
            to = rule(x, y)
            if to is not None:
                pairs.append((4 * y + x, 4 * (to[1] % 4) + to[0] % 4))
    return lax.ppermute(value, "p", pairs)


def start_exchange(own):
    up = move(own, lambda x, y: (x, y + 1))
    down = move(own, lambda x, y: (x, y - 1))
    across = move(own, lambda x, y: (x + 2, y))
    return up, down, across


def end_exchange(own, up, down, across, turned):
    eight = move(turned, lambda x, y: (x, y - 1) if x < 2 else (x, y + 1))
    aslant = move(across, lambda x, y: (x, y + 1) if x < 2 else (x, y - 1))
    wrap = move(turned, lambda x, y: (3 - x, y) if x in (0, 3) else None)
    left = move(own, lambda x, y: (x + 1, y) if x < 3 else None)
    right = move(own, lambda x, y: (x - 1, y) if x > 0 else None)
    return up, down, eight, across, aslant, wrap, left, right


def slots_of(m, x, zh, p):
    first = lax.dynamic_slice_in_dim(x, zh, 1, axis=0)
    wrap = jnp.clip(zh + jnp.where(p < 8, 1, -1), 0, ZG - 1)
    return jnp.concatenate([first, m, lax.dynamic_slice_in_dim(x, wrap, 1, axis=0)], axis=0)


def gather_heads(packed):
    wide = lax.all_to_all(packed, ("zh", "h"), 0, 0, tiled=True)
    return wide.reshape(4, 4, 2, 2, QTR, E)


def shards(queries, key_vectors, value_vectors, grad_output, block_mask, block_frame):
    zh, p, h = lax.axis_index("zh"), lax.axis_index("p"), lax.axis_index("h")
    pos = jnp.stack([zh, p, h]).astype(jnp.int32)
    rates = turn_rates()
    low = lax.rem(p, 4) < 2
    kv = gather_heads(pack(pos, block_frame, rates, key_vectors, value_vectors))
    qg = pack(pos, block_frame, rates, queries, grad_output)
    kv_own = slots_of(kv[:, :, 0], kv[:, :, 1], zh, p)
    up, down, across = start_exchange(kv_own)
    own5 = kv_own[:5]
    across, down, up, own5 = lax.optimization_barrier((across, down, up, own5))
    kv_parts = end_exchange(own5, up, down, across, jnp.where(low, down, up))
    qg = gather_heads(qg)
    qg_own = slots_of(qg[:, :, 0], qg[:, :, 1], zh, p)
    qg_own, kv_some = lax.optimization_barrier((qg_own, kv_parts[2:6]))
    kv_parts = kv_parts[:2] + tuple(kv_some) + kv_parts[6:]
    up, down, across = start_exchange(qg_own)
    att, stats = forward_side(pos, block_mask, kv, qg, kv_parts)
    turned = jnp.where(low, down, up)
    own, turned, across, att, stats = lax.optimization_barrier(
        (qg_own, turned, across, att, stats)
    )
    qg_parts = end_exchange(own, up, down, across, turned)
    every = lax.all_to_all(
        jnp.broadcast_to(stats[None], (GROUPS, SROWS, E)), ("zh", "p"), 0, 0, tiled=True
    )
    scalars = (pos, block_frame, rates)
    am, ax = query_side(scalars, block_mask, kv, qg, att, stats, kv_parts)
    am, every = lax.optimization_barrier((am, every))
    bm = key_side(scalars, block_mask, kv, qg, every, qg_parts)
    out = lax.all_to_all(am.reshape(16, 2, QTR, E), ("zh", "h"), 0, 0, tiled=True)
    out, bm = lax.optimization_barrier((out, bm))
    pieces = list(extra_key_side(scalars, block_mask, kv, qg, every, ax, qg_parts))
    for n in range(1, 4):
        pieces[n] = lax.ppermute(pieces[n], "h", [(i, (i + n) % 4) for i in range(4)])
    bm = lax.all_to_all(bm.reshape(16, 2, QTR, E), ("zh", "h"), 0, 0, tiled=True)
    return unpack(pos, out, bm, pieces)


def solution(mesh):
    fine = Mesh(mesh.devices.reshape(ZG, PLANE, 4), ("zh", "p", "h"))
    tok = P(("zh", "p", "h"), None, None)
    return jax.shard_map(
        shards,
        mesh=fine,
        in_specs=(tok, tok, tok, tok, P(), P()),
        out_specs=(tok, tok, tok, tok),
        check_vma=False,
    )
```

```python
import functools
import math

import jax
import jax.numpy as jnp
import numpy as np
from jax import lax
from jax.experimental import pallas as pl
from jax.experimental.pallas import tpu as pltpu
from jax.sharding import Mesh, PartitionSpec as P

ROT = 44
HALF = ROT // 2
BLK = 128
E = 128
TOK = 256
QTR = 64
GROUPS = 64
PLANE = 16
ZG = 4
UNITS = 5
SROWS = 24
NEG = -1e30
PARTS = 8
OFFSETS = (0, 16, -16, 32, -32, 4, -4, 8, -8, 1, -1, 2, -2)
FIRST_FAR = 4
SLOTS = 48
SCALE = 1.0 / math.sqrt(E)
LOG2E = 1.4426950408889634
COEF = SCALE * LOG2E
F32 = jnp.float32
BF16 = jnp.bfloat16
HBM = pl.BlockSpec(memory_space=pltpu.HBM)
SMEM = pl.BlockSpec(memory_space=pltpu.SMEM)
VMEM = pl.BlockSpec(memory_space=pltpu.VMEM)

WIDE = jax.ShapeDtypeStruct((16, 2, 2, QTR, E), BF16)


def dot(a, b, ca, cb):
    return lax.dot_general(a, b, (((ca,), (cb,)), ((), ())), preferred_element_type=F32)


def turn(x, c, s1, s2):
    return x * c + pltpu.roll(x, HALF, x.ndim - 1) * s1 + pltpu.roll(x, E - HALF, x.ndim - 1) * s2


def pack_kernel(pos, frames, rates, a_hbm, b_hbm, o_ref, a_ref, b_ref, sems):
    copies = [
        pltpu.make_async_copy(a_hbm, a_ref, sems.at[0]),
        pltpu.make_async_copy(b_hbm, b_ref, sems.at[1]),
    ]
    for copy in copies:
        copy.start()
    block = 2 * (pos[0] * PLANE + pos[1]) + pos[2] // 2
    rows = [r[None] for r in turn_rows(frames, rates, block)]
    copies[0].wait()
    a = turn(a_ref[...].astype(F32), *rows).astype(BF16)
    copies[1].wait()
    for n, val in ((0, a), (1, b_ref[...])):
        o_ref[:, 0, n] = val[:16]
        for i in range(4):
            o_ref[4 * i : 4 * i + 4, 1, n] = val[16:]


def pack(pos, frames, rates, *tensors):
    return pl.pallas_call(
        pack_kernel,
        out_shape=WIDE,
        in_specs=[SMEM, SMEM, VMEM, HBM, HBM],
        out_specs=VMEM,
        scratch_shapes=[
            pltpu.VMEM((20, QTR, E), BF16),
            pltpu.VMEM((20, QTR, E), BF16),
            pltpu.SemaphoreType.DMA((2,)),
        ],
        compiler_params=LIMIT,
        name="pack",
    )(pos, frames, rates, *[jnp.transpose(t, (1, 0, 2)) for t in tensors])


def unpack_kernel(pos, a_hbm, b_hbm, *refs):
    pieces, outs, sems = refs[:4], refs[4:8], refs[8]
    copies = []
    for i, o in enumerate(outs):
        main = (a_hbm, b_hbm)[i // 2]
        copies.append(
            pltpu.make_async_copy(main.at[:, i % 2], o.at[pl.ds(0, 16)], sems.at[5 * i])
        )
        for n, piece in enumerate(pieces):
            to = 16 + lax.rem(pos[2] - n + 4, 4)
            copies.append(pltpu.make_async_copy(piece.at[i], o.at[to], sems.at[5 * i + n + 1]))
    for copy in copies:
        copy.start()
    for copy in copies:
        copy.wait()


def unpack(pos, a, b, pieces):
    shape = jax.ShapeDtypeStruct((20, QTR, E), BF16)
    outs = pl.pallas_call(
        unpack_kernel,
        out_shape=(shape,) * 4,
        in_specs=[SMEM] + [pl.BlockSpec(memory_space=pl.ANY)] * 6,
        out_specs=(HBM,) * 4,
        scratch_shapes=[pltpu.SemaphoreType.DMA((20,))],
        compiler_params=pltpu.CompilerParams(vmem_limit_bytes=2**20),
        name="unpack",
    )(pos, a, b, *pieces)
    return tuple(jnp.transpose(o, (1, 0, 2)) for o in outs)


def source(offset, unit, zh, p):
    is_x = unit == 4
    z = jnp.where(is_x, zh, unit)
    group = z * PLANE + p
    other = group - offset
    valid = (other >= 0) & (other < GROUPS)
    if local(offset):
        slot = jnp.clip(z - offset // PLANE, 0, ZG - 1)
    else:
        x = lax.rem(p, 4)
        low = x < 2
        base = {
            4: lambda: 0,
            -4: lambda: 6,
            8: lambda: 12,
            -8: lambda: 12,
            1: lambda: jnp.where(x == 0, 30, 36),
            -1: lambda: jnp.where(x == 3, 30, 42),
            2: lambda: jnp.where(low, 24, 18),
            -2: lambda: jnp.where(low, 18, 24),
        }[offset]()
        at = p - offset
        step = jnp.where(at < 0, -1, jnp.where(at >= PLANE, 1, 0))
        zz = jnp.clip(z + step, 0, ZG - 1)
        slot = base + jnp.where(is_x, 5 * step * step, 1 + zz)
    return group, jnp.clip(other, 0, GROUPS - 1), valid, slot


def local(offset):
    return offset == 0 or abs(offset) >= PLANE


def add_bias(st, bias):
    top = jnp.concatenate([st[:BLK, :BLK] + bias[0][0], st[:BLK, BLK:] + bias[0][1]], axis=1)
    low = jnp.concatenate([st[BLK:, :BLK] + bias[1][0], st[BLK:, BLK:] + bias[1][1]], axis=1)
    return jnp.concatenate([top, low], axis=0)


def bias_of(mask, q_group, k_group, valid):
    return [
        [
            jnp.where(valid & (mask[2 * q_group + qb, 2 * k_group + kb] != 0), 0.0, NEG)
            for qb in range(2)
        ]
        for kb in range(2)
    ]


def fetch(parts, pool, sems, wholes=(), only_x=False):
    copies = []
    for n, ref in enumerate(parts):
        at = 6 * n
        size = ref.shape[0]
        for first, count in (((0, 1), (5, 1)) if only_x else ((0, size),)):
            if first < size:
                copies.append(
                    pltpu.make_async_copy(
                        ref.at[pl.ds(first, count)],
                        pool.at[pl.ds(at + first, count)],
                        sems.at[2 * n + (first > 0)],
                    )
                )
    for n, (whole, target) in enumerate(wholes):
        copies.append(pltpu.make_async_copy(whole, target, sems.at[2 * PARTS + n]))
    far_count = len(copies) - len(wholes)
    for copy in copies[far_count:] + copies[:far_count]:
        copy.start()
    for copy in copies[far_count:]:
        copy.wait()

    def rest():
        for copy in copies[:far_count]:
            copy.wait()

    return rest


def near(ref, z, unit, which):
    return ref[z, :, jnp.where(unit == 4, 1, 0), which].reshape(TOK, E)


def far(ref, slot, which):
    return ref[slot, :, which].reshape(TOK, E)


def turn_rows(frames, rates, block):
    angles = frames[block].astype(F32) * rates[0:1]
    sine = jnp.sin(angles)
    return jnp.cos(angles), sine * rates[1:2], sine * rates[2:3]


def unturn(x, frames, rates, group):
    halves = []
    for blk in range(2):
        c, s1, s2 = turn_rows(frames, rates, 2 * group + blk)
        halves.append(turn(x[blk * BLK : (blk + 1) * BLK], c, -s1, -s2))
    return jnp.concatenate(halves, axis=0)


def put(ref, at, which, val):
    for b in range(4):
        ref[at, b, which] = val[b * QTR : (b + 1) * QTR]


def read_stats(ref, unit, *at):
    rows = [ref[(*at, pl.ds(4 * unit + n, 1), slice(None))] for n in range(4)]
    return jnp.concatenate(rows[:2], axis=1), jnp.concatenate(rows[2:], axis=1)


def pool_rows(offset, slot, unit, near_ref, pool, which):
    if local(offset):
        return near(near_ref, slot, unit, which)
    return far(pool, slot, which)


def forward_kernel(pos, *refs):
    parts, wholes, others = refs[:PARTS], refs[PARTS : PARTS + 3], refs[PARTS + 3 :]
    att_ref, stats, pool, sems, mask, kv, qg, scores, weights, values = others
    rest = fetch(parts, pool, sems, list(zip(wholes, (mask, kv, qg))))
    zh, p = pos[0], pos[1]

    def body(unit, carry):
        z = jnp.where(unit == 4, zh, unit)
        q = near(qg, z, unit, 0)
        slots = []
        top = jnp.full((1, TOK), NEG, F32)
        for n, offset in enumerate(OFFSETS):
            if offset == FIRST_FAR:
                pl.when(unit == 0)(rest)
            group, other, valid, slot = source(offset, unit, zh, p)
            slots.append(slot)
            k = pool_rows(offset, slot, unit, kv, pool, 0)
            st = add_bias(dot(k, q, 1, 1), bias_of(mask, group, other, valid))
            scores[n] = st
            top = jnp.maximum(top, jnp.max(st, axis=0, keepdims=True))
        top = top * COEF
        total = jnp.zeros((1, TOK), F32)
        for n, offset in enumerate(OFFSETS):
            w = jnp.exp2(scores[n] * COEF - top)
            total = total + jnp.sum(w, axis=0, keepdims=True)
            rows = slice(n * TOK, (n + 1) * TOK)
            weights[rows] = w.astype(BF16)
            values[rows] = pool_rows(offset, slots[n], unit, kv, pool, 1)
        out = dot(values[...], weights[...], 0, 0)
        att = jnp.transpose(out * (1.0 / total)).astype(BF16)
        put(att_ref, unit, 0, att)
        g = near(qg, z, unit, 1).astype(F32)
        delta = jnp.sum(jnp.transpose(g * att.astype(F32)), axis=0, keepdims=True)
        for n, row in enumerate((top + jnp.log2(total), delta)):
            stats[pl.ds(4 * unit + 2 * n, 1), :] = row[:, :BLK]
            stats[pl.ds(4 * unit + 2 * n + 1, 1), :] = row[:, BLK:]
        return carry

    stats[...] = jnp.zeros_like(stats)
    lax.fori_loop(0, UNITS, body, 0)


def query_kernel(pos, frames, rates, *refs):
    parts, wholes, others = refs[:PARTS], refs[PARTS : PARTS + 5], refs[PARTS + 5 :]
    m_ref, x_ref, pool, sems, mask, kv, qg, att, stats, dscores, keys, values, scores, products = others
    rest = fetch(parts, pool, sems, list(zip(wholes, (mask, kv, qg, att, stats))))
    zh, p = pos[0], pos[1]

    def body(unit, carry):
        z = jnp.where(unit == 4, zh, unit)
        q = near(qg, z, unit, 0)
        g = near(qg, z, unit, 1)
        total, delta = read_stats(stats, unit)
        for n, offset in enumerate(OFFSETS):
            if offset == FIRST_FAR:
                pl.when(unit == 0)(rest)
            slot = source(offset, unit, zh, p)[3]
            keys[n * TOK : (n + 1) * TOK] = pool_rows(offset, slot, unit, kv, pool, 0)
            values[n * TOK : (n + 1) * TOK] = pool_rows(offset, slot, unit, kv, pool, 1)
        scores[...] = dot(keys[...], q, 1, 1)
        products[...] = dot(values[...], g, 1, 1)
        for n, offset in enumerate(OFFSETS):
            group, other, valid, _ = source(offset, unit, zh, p)
            rows = slice(n * TOK, (n + 1) * TOK)
            st = add_bias(scores[rows], bias_of(mask, group, other, valid))
            w = jnp.exp2(st * COEF - total)
            dscores[rows] = (w * (products[rows] - delta)).astype(BF16)
        dq = dot(keys[...], dscores[...], 0, 0)
        dq = unturn(jnp.transpose(dq * SCALE), frames, rates, z * PLANE + p).astype(BF16)

        @pl.when(unit < 4)
        def _():
            m_ref[unit, :, 0] = att[unit, :, 0]
            put(m_ref, unit, 1, dq)

        @pl.when(unit == 4)
        def _():
            x_ref[0, :, 0] = att[4, :, 0]
            put(x_ref, 0, 1, dq)

        return carry

    lax.fori_loop(0, UNITS, body, 0)


def key_terms(unit, zh, p, mask, kv, qg, pool, stats_of, rest, big):
    z = jnp.where(unit == 4, zh, unit)
    k = near(kv, z, unit, 0)
    v = near(kv, z, unit, 1)
    weights, dscores, queries, grads, scores, products = big
    for n, offset in enumerate(OFFSETS):
        if offset == FIRST_FAR:
            rest()
        slot = source(offset, unit, zh, p)[3]
        cols = slice(n * TOK, (n + 1) * TOK)
        queries[cols] = pool_rows(offset, slot, unit, qg, pool, 0)
        grads[cols] = pool_rows(offset, slot, unit, qg, pool, 1)
    scores[...] = dot(k, queries[...], 1, 1)
    products[...] = dot(v, grads[...], 1, 1)
    for n, offset in enumerate(OFFSETS):
        group, other, valid, _ = source(offset, unit, zh, p)
        total, delta = stats_of(other)
        cols = slice(n * TOK, (n + 1) * TOK)
        st = add_bias(scores[:, cols], bias_of(mask, other, group, valid))
        w = jnp.exp2(st * COEF - total)
        weights[:, cols] = w.astype(BF16)
        dscores[:, cols] = (w * (products[:, cols] - delta)).astype(BF16)
    return dot(dscores[...], queries[...], 1, 0), dot(weights[...], grads[...], 1, 0)


def key_kernel(pos, frames, rates, *refs):
    parts, wholes, others = refs[:PARTS], refs[PARTS : PARTS + 4], refs[PARTS + 4 :]
    o_ref, pool, sems, mask, kv, qg, stats, *big = others
    rest = fetch(parts, pool, sems, list(zip(wholes, (mask, kv, qg, stats))))
    zh, p = pos[0], pos[1]

    def stats_of(other):
        return read_stats(stats, lax.div(other, PLANE), zh * PLANE + lax.rem(other, PLANE))

    def body(unit, carry):
        dk, dv = key_terms(
            unit, zh, p, mask, kv, qg, pool, stats_of, lambda: pl.when(unit == 0)(rest), big
        )
        dk = unturn(dk * SCALE, frames, rates, unit * PLANE + p)
        put(o_ref, unit, 0, dk.astype(BF16))
        put(o_ref, unit, 1, dv.astype(BF16))
        return carry

    lax.fori_loop(0, ZG, body, 0)


def extra_key_kernel(pos, frames, rates, *refs):
    parts, wholes, others = refs[:PARTS], refs[PARTS : PARTS + 5], refs[PARTS + 5 :]
    pieces, (pool, sems, mask, kv, qg, stats, done, *big, sums) = others[:4], others[4:]
    rest = fetch(parts, pool, sems, list(zip(wholes, (mask, kv, qg, stats, done))), only_x=True)
    zh, p, h = pos[0], pos[1], pos[2]

    def stats_of(other):
        return read_stats(stats, 4, other)

    dk, dv = key_terms(jnp.int32(4), zh, p, mask, kv, qg, pool, stats_of, rest, big)
    put(sums, 0, 0, unturn(dk * SCALE, frames, rates, zh * PLANE + p).astype(BF16))
    put(sums, 0, 1, dv.astype(BF16))
    for n, piece in enumerate(pieces):
        to = lax.rem(h + n, 4)
        for i in range(2):
            piece[i] = done[0, to, i]
            piece[2 + i] = sums[0, to, i]


def cost(pairs, products):
    return pl.CostEstimate(
        flops=pairs * products * 2 * TOK * TOK * E,
        bytes_accessed=8 * 2**20,
        transcendentals=pairs * TOK * TOK,
    )


LIMIT = pltpu.CompilerParams(vmem_limit_bytes=60 * 2**20)


POOL = [
    pltpu.VMEM((SLOTS, 4, 2, QTR, E), BF16),
    pltpu.SemaphoreType.DMA((2 * PARTS + 5,)),
    pltpu.SMEM((2 * GROUPS, 2 * GROUPS), jnp.int32),
    pltpu.VMEM((4, 4, 2, 2, QTR, E), BF16),
    pltpu.VMEM((4, 4, 2, 2, QTR, E), BF16),
]
ALL_SUMS = pltpu.VMEM((len(OFFSETS) * TOK, TOK), F32)
ALL_PAIRS = pltpu.VMEM((len(OFFSETS) * TOK, TOK), BF16)
ALL_ROWS = pltpu.VMEM((len(OFFSETS) * TOK, E), BF16)
ALL_COLUMNS = pltpu.VMEM((TOK, len(OFFSETS) * TOK), BF16)
WIDE_SUMS = pltpu.VMEM((TOK, len(OFFSETS) * TOK), F32)
BIG = [ALL_COLUMNS, ALL_COLUMNS, ALL_ROWS, ALL_ROWS, WIDE_SUMS, WIDE_SUMS]
EVERY = pltpu.VMEM((GROUPS, SROWS, E), F32)


def side(kernel, out_shape, scratch, pairs, products, scalars, arrays):
    outs = out_shape if isinstance(out_shape, tuple) else (out_shape,)
    specs = [SMEM, SMEM, VMEM][: len(scalars)]
    return pl.pallas_call(
        kernel,
        out_shape=out_shape,
        in_specs=specs + [HBM] * len(arrays),
        out_specs=(VMEM,) * len(outs) if isinstance(out_shape, tuple) else VMEM,
        scratch_shapes=POOL + scratch,
        compiler_params=LIMIT,
        cost_estimate=cost(pairs, products),
        name=kernel.__name__,
    )(*scalars, *arrays)


def blocks(units, tensors):
    return jax.ShapeDtypeStruct((units, 4, tensors, QTR, E), BF16)


def forward_side(pos, mask, kv, qg, parts):
    shapes = (blocks(UNITS, 1), jax.ShapeDtypeStruct((SROWS, E), F32))
    scratch = [pltpu.VMEM((len(OFFSETS), TOK, TOK), F32), ALL_PAIRS, ALL_ROWS]
    return side(forward_kernel, shapes, scratch, 65, 2, (pos,), (*parts, mask, kv, qg))


def query_side(scalars, mask, kv, qg, att, stats, parts):
    scratch = [pltpu.VMEM((UNITS, 4, 1, QTR, E), BF16), pltpu.VMEM((SROWS, E), F32)]
    scratch += [ALL_PAIRS, ALL_ROWS, ALL_ROWS, ALL_SUMS, ALL_SUMS]
    arrays = (*parts, mask, kv, qg, att, stats)
    return side(query_kernel, (blocks(ZG, 2), blocks(1, 2)), scratch, 65, 3, scalars, arrays)


def key_side(scalars, mask, kv, qg, stats, parts):
    return side(
        key_kernel, blocks(ZG, 2), [EVERY] + BIG, 52, 4, scalars, (*parts, mask, kv, qg, stats)
    )


def extra_key_side(scalars, mask, kv, qg, stats, done, parts):
    pieces = (jax.ShapeDtypeStruct((4, QTR, E), BF16),) * 4
    pair = pltpu.VMEM((1, 4, 2, QTR, E), BF16)
    arrays = (*parts, mask, kv, qg, stats, done)
    return side(extra_key_kernel, pieces, [EVERY, pair] + BIG + [pair], 13, 4, scalars, arrays)


def turn_rates():
    rates = np.zeros((8, E), np.float32)
    rates[0, :HALF] = 10000.0 ** (-2.0 * np.arange(HALF, dtype=np.float32) / ROT)
    rates[0, HALF:ROT] = rates[0, :HALF]
    rates[1, HALF:ROT] = 1.0
    rates[2, :HALF] = -1.0
    return rates


def move(value, rule):
    pairs = []
    for y in range(4):
        for x in range(4):
            to = rule(x, y)
            if to is not None:
                pairs.append((4 * y + x, 4 * (to[1] % 4) + to[0] % 4))
    return lax.ppermute(value, "p", pairs)


def start_exchange(own):
    up = move(own, lambda x, y: (x, y + 1))
    down = move(own, lambda x, y: (x, y - 1))
    across = move(own, lambda x, y: (x + 2, y))
    return up, down, across


def end_exchange(own, up, down, across, turned):
    eight = move(turned, lambda x, y: (x, y - 1) if x < 2 else (x, y + 1))
    aslant = move(across, lambda x, y: (x, y + 1) if x < 2 else (x, y - 1))
    wrap = move(turned, lambda x, y: (3 - x, y) if x in (0, 3) else None)
    left = move(own, lambda x, y: (x + 1, y) if x < 3 else None)
    right = move(own, lambda x, y: (x - 1, y) if x > 0 else None)
    return up, down, eight, across, aslant, wrap, left, right


def slots_of(m, x, zh, p):
    first = lax.dynamic_slice_in_dim(x, zh, 1, axis=0)
    wrap = jnp.clip(zh + jnp.where(p < 8, 1, -1), 0, ZG - 1)
    return jnp.concatenate([first, m, lax.dynamic_slice_in_dim(x, wrap, 1, axis=0)], axis=0)


def gather_heads(packed):
    wide = lax.all_to_all(packed, ("zh", "h"), 0, 0, tiled=True)
    return wide.reshape(4, 4, 2, 2, QTR, E)


def shards(queries, key_vectors, value_vectors, grad_output, block_mask, block_frame):
    zh, p, h = lax.axis_index("zh"), lax.axis_index("p"), lax.axis_index("h")
    pos = jnp.stack([zh, p, h]).astype(jnp.int32)
    rates = turn_rates()
    low = lax.rem(p, 4) < 2
    kv = gather_heads(pack(pos, block_frame, rates, key_vectors, value_vectors))
    qg = pack(pos, block_frame, rates, queries, grad_output)
    kv_own = slots_of(kv[:, :, 0], kv[:, :, 1], zh, p)
    up, down, across = start_exchange(kv_own)
    own5 = kv_own[:5]
    across, down, up, own5 = lax.optimization_barrier((across, down, up, own5))
    kv_parts = end_exchange(own5, up, down, across, jnp.where(low, down, up))
    qg = gather_heads(qg)
    qg_own = slots_of(qg[:, :, 0], qg[:, :, 1], zh, p)
    qg_own, kv_some = lax.optimization_barrier((qg_own, kv_parts[2:6]))
    kv_parts = kv_parts[:2] + tuple(kv_some) + kv_parts[6:]
    up, down, across = start_exchange(qg_own)
    att, stats = forward_side(pos, block_mask, kv, qg, kv_parts)
    turned = jnp.where(low, down, up)
    own, turned, across, att, stats = lax.optimization_barrier(
        (qg_own, turned, across, att, stats)
    )
    qg_parts = end_exchange(own, up, down, across, turned)
    every = lax.all_to_all(
        jnp.broadcast_to(stats[None], (GROUPS, SROWS, E)), ("zh", "p"), 0, 0, tiled=True
    )
    scalars = (pos, block_frame, rates)
    am, ax = query_side(scalars, block_mask, kv, qg, att, stats, kv_parts)
    am, every = lax.optimization_barrier((am, every))
    bm = key_side(scalars, block_mask, kv, qg, every, qg_parts)
    out = lax.all_to_all(am.reshape(16, 2, QTR, E), ("zh", "h"), 0, 0, tiled=True)
    out, bm = lax.optimization_barrier((out, bm))
    pieces = list(extra_key_side(scalars, block_mask, kv, qg, every, ax, qg_parts))
    for n in range(1, 4):
        pieces[n] = lax.ppermute(pieces[n], "h", [(i, (i + n) % 4) for i in range(4)])
    bm = lax.all_to_all(bm.reshape(16, 2, QTR, E), ("zh", "h"), 0, 0, tiled=True)
    return unpack(pos, out, bm, pieces)


def solution(mesh):
    fine = Mesh(mesh.devices.reshape(ZG, PLANE, 4), ("zh", "p", "h"))
    tok = P(("zh", "p", "h"), None, None)
    return jax.shard_map(
        shards,
        mesh=fine,
        in_specs=(tok, tok, tok, tok, P(), P()),
        out_specs=(tok, tok, tok, tok),
        check_vma=False,
    )
```
